128 devices in a mesh: dp: 32 (over z, y, x_hi), expert: 4 (over x_lo, core).
Axes of the slice: x: 4 (x_hi: 2, x_lo: 2; x = x_hi * 2 + x_lo), y: 4, z: 4, core: 2. Of those that a mesh axis runs over, the one named last changes fastest.
Arguments:
- resid: bfloat16 [16384, 2048], P(('dp', 'expert')), may hold values from -6 to 6
- norm_gain: float32 [2048], replicated, may hold values from 0.25 to 1.75
- w_gate: bfloat16 [128, 2048, 768], P(('dp', 'expert')), may hold values from -0.125 to 0.125
- w_up: bfloat16 [128, 2048, 768], P(('dp', 'expert')), may hold values from -0.125 to 0.125
- w_down: bfloat16 [128, 768, 2048], P(('dp', 'expert')), may hold values from -0.21875 to 0.21875
- route_ids: int32 [16384, 8], P(('dp', 'expert')), may hold values from 0 to 127, as said below
- route_slots: int32 [16384, 8], P(('dp', 'expert')), may hold values from -1 to 19, as said below
- route_weights: float32 [16384, 8], P(('dp', 'expert')), may hold values from 0.02 to 0.5
Outputs:
- stream_out: bfloat16 [16384, 2048], P(('dp', 'expert'))
The draws below stay inside these ranges and needn't reach their ends.
Inputs may be any that keep to these rules, and one draw needn't show every extreme that they name: `route_ids`: each row names 8 different experts. `route_slots`: -1 marks a dropped choice. Among the rows of one device, the kept choices of one expert hold the slots 0, 1, 2, ... without repeats. Three experts, the same for all devices, have slots below 20; all others have slots below 10. On every device each of those three fills all 20 of its slots and some other expert fills all 10.
All inputs are finite; a program needn't handle non-finite values.
Results may differ from the reference program's by a relative error of at most 0.0044.
Values may be sent and summed in bfloat16 or wider, within the bound.
A program may use at most 128 MiB of HBM per device.

```python
import math
import jax
import jax.numpy as jnp
from jax import lax

D = 2048
FF = 768
ROUTE_FANOUT = 8
TOKENS_PER_SHARD = 128
EXPERT_TOTAL = 128
TOKENS = 16384
CAP = 10
CAP_HOT = 20
HOT_LOAD = 30
N_DP = 32
N_EXPERT = 4


def route_tables(key):
    token_groups = N_DP * N_EXPERT
    expert_line = jnp.arange(EXPERT_TOTAL, dtype=jnp.int32)
    layer_key = jax.random.fold_in(key, 40)
    key_order, key_score, key_hot, key_warm, key_pick = jax.random.split(layer_key, 5)
    order = jax.random.permutation(key_order, EXPERT_TOTAL).astype(jnp.int32)
    hot_list = order[:3]
    router_scores = jax.random.randint(key_score, (token_groups, TOKENS_PER_SHARD, EXPERT_TOTAL), 0, 4096, dtype=jnp.int32) * EXPERT_TOTAL + expert_line
    hot_keys = jax.random.split(key_hot, 3 * token_groups)
    hot_ranks = jax.vmap(lambda one_key: jax.random.permutation(one_key, TOKENS_PER_SHARD))(hot_keys).reshape(3, token_groups, TOKENS_PER_SHARD)
    score_boost = jnp.zeros((token_groups, TOKENS_PER_SHARD, EXPERT_TOTAL), jnp.int32)
    for hot_slot in range(3):
        pinned_choice = (hot_ranks[hot_slot] < HOT_LOAD).astype(jnp.int32)
        expert_column = (expert_line == hot_list[hot_slot]).astype(jnp.int32)
        score_boost = score_boost + pinned_choice[:, :, None] * expert_column[None, None, :] * 16777216
    warm_pick = jax.random.randint(key_pick, (token_groups,), 0, EXPERT_TOTAL - 3, dtype=jnp.int32)
    warm_expert = order[3 + warm_pick]
    warm_keys = jax.random.split(key_warm, token_groups)
    warm_ranks = jax.vmap(lambda one_key: jax.random.permutation(one_key, TOKENS_PER_SHARD))(warm_keys)
    heated_pinned = (warm_ranks < CAP).astype(jnp.int32)
    heated_column = (expert_line[None, :] == warm_expert[:, None]).astype(jnp.int32)
    score_boost = score_boost + heated_pinned[:, :, None] * heated_column[:, None, :] * 16777216
    unused_value, selected_experts = lax.top_k(router_scores + score_boost, ROUTE_FANOUT)
    selected_experts = selected_experts.astype(jnp.int32)
    flat = selected_experts.reshape(token_groups, TOKENS_PER_SHARD * ROUTE_FANOUT)
    onehot = (flat[:, :, None] == expert_line[None, None, :]).astype(jnp.int32)
    ranks = jnp.sum(jnp.cumsum(onehot, axis=1) * onehot, axis=2) - 1
    is_hot = jnp.any(flat[:, :, None] == hot_list[None, None, :], axis=2)
    capacity = jnp.where(is_hot, CAP_HOT, CAP)
    slots = jnp.where(ranks < capacity, ranks, -1).astype(jnp.int32)
    return (selected_experts.reshape(TOKENS, ROUTE_FANOUT), slots.reshape(TOKENS, ROUTE_FANOUT))


def draw_route_ids(key, part):
    return route_tables(key)[0]


def draw_route_slots(key, part):
    return route_tables(key)[1]


def block_levels(own_key, dims, cuts, least, high):
    gain = 1.0
    for dim, blocks in cuts:
        steps = jax.random.uniform(jax.random.fold_in(jax.random.fold_in(own_key, 6), dim), (blocks,), jnp.float32, least / len(cuts), high / len(cuts))
        gain = gain * jnp.repeat(jnp.exp(steps), dims[dim] // blocks).reshape((-1,) + (1,) * (len(dims) - 1 - dim))
    return gain


def scatter_about(stream_key, shape, scale, limit, cuts=(), kind=jnp.bfloat16):
    array = scale * jax.random.normal(stream_key, shape, jnp.float32)
    if cuts:
        array = array * block_levels(stream_key, shape, cuts, -0.22, 0.18)
    return jnp.clip(array, -limit, limit).astype(kind)


def setup_inputs(seed: int = 0) -> dict:
    splits = jax.random.split(jax.random.key(seed), 9)
    return {
        "resid": scatter_about(splits[0], (TOKENS, D), 1.0, 6.0, ((0, 128),)),
        "norm_gain": jnp.clip(1.0 + 0.15 * jax.random.normal(splits[1], (D,), jnp.float32), 0.25, 1.75),
        "w_gate": scatter_about(splits[2], (EXPERT_TOTAL, D, FF), D ** -0.5, 0.125, ((0, 128),)),
        "w_up": scatter_about(splits[3], (EXPERT_TOTAL, D, FF), D ** -0.5, 0.125, ((0, 128),)),
        "w_down": scatter_about(splits[4], (EXPERT_TOTAL, FF, D), FF ** -0.5, 0.21875, ((0, 128),)),
        "route_ids": draw_route_ids(jax.random.fold_in(splits[8], 71), 0),
        "route_slots": draw_route_slots(jax.random.fold_in(splits[8], 71), 0),
        "route_weights": jnp.clip(jnp.exp(math.log(0.5) - 3.218876 * jax.random.uniform(splits[7], (TOKENS, ROUTE_FANOUT), jnp.float32) ** block_levels(splits[7], (TOKENS, ROUTE_FANOUT), ((0, 128),), -0.2, 0.2)), 0.02, 0.5),
    }


epsilon = 1e-06

def reference(resid, norm_gain, w_gate, w_up, w_down, route_ids, route_slots, route_weights):
    floats = resid.astype(jnp.float32)
    mean_square = lax.optimization_barrier(jnp.mean(floats * floats, axis=1, keepdims=True))
    normed = (floats * lax.rsqrt(mean_square + epsilon) * norm_gain[None, :]).astype(jnp.bfloat16)
    device_of = (jnp.arange(TOKENS, dtype=jnp.int32) // TOKENS_PER_SHARD).astype(jnp.int32)
    retained = route_slots >= 0
    slot_row = (device_of[:, None] * CAP_HOT + route_slots).astype(jnp.int32)
    expert_row = jnp.where(retained, route_ids, EXPERT_TOTAL).astype(jnp.int32)
    token_grid = jnp.broadcast_to(jnp.arange(TOKENS, dtype=jnp.int32)[:, None], route_ids.shape)
    row_count = N_DP * N_EXPERT * CAP_HOT
    row_tokens = jnp.full((EXPERT_TOTAL, row_count), TOKENS, jnp.int32).at[expert_row, slot_row].set(token_grid, mode='drop')
    row_weights = jnp.zeros((EXPERT_TOTAL, row_count), jnp.float32).at[expert_row, slot_row].set(route_weights, mode='drop')
    padded = jnp.concatenate([normed, jnp.zeros((1, D), jnp.bfloat16)], axis=0)

    def expert_step(totals, packed):
        token_index, weight_row, gate_matrix, up_matrix, down_matrix = packed
        rows = padded[token_index]
        gate_sum = jnp.dot(rows, gate_matrix, preferred_element_type=jnp.float32)
        up_sum = jnp.dot(rows, up_matrix, preferred_element_type=jnp.float32)
        hidden = (jax.nn.silu(gate_sum) * up_sum).astype(jnp.bfloat16)
        outputs = jnp.dot(hidden, down_matrix, preferred_element_type=jnp.float32).astype(jnp.bfloat16)
        totals = totals.at[token_index].add(weight_row[:, None] * outputs.astype(jnp.float32))
        return (totals, None)
    start_totals = jnp.zeros((TOKENS + 1, D), jnp.float32)
    totals, unused_value = lax.scan(expert_step, start_totals, (row_tokens, row_weights, w_gate, w_up, w_down))
    return (floats + totals[:TOKENS]).astype(jnp.bfloat16)
```

```python
import jax
import jax.numpy as jnp
from jax import lax
from jax.experimental import pallas as pl
from jax.experimental.pallas import tpu as pltpu
from jax.sharding import PartitionSpec as P

MESH = pl.DeviceIdType.MESH
F32 = jnp.float32
BF16 = jnp.bfloat16
epsilon = 1e-06

TOK = 128
D = 2048
FF = 768
FAN = 8
CAP = 20
PAIR = 2 * CAP
WAYS = ((2, 1, 0), (0, 2, 1), (1, 0, 2))
WIDTH = (384, 384, 256)
START = (0, 384, 768)
HALF = 1024
LANES = 384
ROWS = 8 * PAIR


def my_place():
    dp = lax.axis_index("dp")
    ex = lax.axis_index("expert")
    return [(dp % 2) * 2 + ex // 2, (dp // 2) % 4, dp // 8], ex % 2


def device(place, core):
    x, y, z = place
    return (z * 8 + y * 2 + x // 2, (x % 2) * 2 + core)


def moved(place, axis, step):
    place = list(place)
    place[axis] = (place[axis] + step) % 4
    return place


def kernel(resid, gain, ids, slots, wts, wg_hbm, wu_hbm, wd_hbm, out,
           tok0, tok1, tok2, g0, g1, g2, r0, r1, r2, x0, x1, x2, a0, a1_, a2_, b0, b1, b2,
           tab, tab1, tab2s, tab2, hidden, wg, wu, wd,
           sem_w, s1s, s1r, t1s, t1r, s2s, s2r, t2s, t2r, s3s, s3r, ras, rar, rbs, rbr, rcs, rcr, q2s, q2r, q1s, q1r, free):
    place, core = my_place()
    toks, gs, rs, xs = (tok0, tok1, tok2), (g0, g1, g2), (r0, r1, r2), (x0, x1, x2)
    acc2, acc1 = (a0, a1_, a2_), (b0, b1, b2)

    def remote(src, dst, ssem, rsem, where, c):
        return pltpu.make_async_remote_copy(
            src_ref=src, dst_ref=dst, send_sem=ssem, recv_sem=rsem,
            device_id=device(where, c), device_id_type=MESH,
        )

    loads = [pltpu.make_async_copy(h, v, sem_w.at[i]) for i, (h, v) in enumerate(((wg_hbm, wg), (wu_hbm, wu), (wd_hbm, wd)))]
    for cp in loads:
        cp.start()

    barrier = pltpu.get_barrier_semaphore()
    for axis in range(3):
        for step in (1, 2, 3):
            for c in range(2):
                pl.semaphore_signal(barrier, inc=1, device_id=device(moved(place, axis, step), c), device_id_type=MESH)
    pl.semaphore_signal(barrier, inc=1, device_id=device(place, 1 - core), device_id_type=MESH)

    floats = resid[...].astype(F32)
    mean_square = jnp.mean(floats * floats, axis=1, keepdims=True)
    normed = (floats * lax.rsqrt(mean_square + epsilon) * gain[...]).astype(BF16)
    for o in range(3):
        for h in range(2):
            lo = h * HALF + START[o]
            toks[o][h] = normed[:, lo:lo + WIDTH[o]]

    pl.semaphore_wait(barrier, 19)

    def first(o, step, cc):
        one, two, _ = WAYS[o]
        h = (core + cc) % 2
        return remote(
            toks[o].at[h], gs[o].at[place[two], place[one], core],
            s1s.at[o, step, cc], s1r.at[o, step, cc], moved(place, one, step), h,
        )

    for step in (1, 3, 2, 0):
        for o in range(3):
            for cc in range(2):
                if step or cc:
                    first(o, step, cc).start()
    for o in range(3):
        one, two, _ = WAYS[o]
        gs[o][place[two], place[one], core] = toks[o][core]

    e = ids[...]
    coords = ((e >> 1) & 3, (e >> 3) & 3, e >> 5)
    sl = slots[...]
    lane = lax.broadcasted_iota(jnp.int32, (TOK, LANES), 1)
    lane128 = lax.broadcasted_iota(jnp.int32, (TOK, 128), 1)
    number = (lax.broadcasted_iota(jnp.int32, (TOK, 1), 0) + 1 + core * TOK).astype(F32)
    weight = wts[...]
    for o in range(3):
        one, two, three = WAYS[o]
        spot = jnp.where(sl >= 0, ((coords[three] * 2 + (e & 1)) * 2 + core) * CAP + sl, -1)
        line = coords[one] * 8 + coords[two]
        total = jnp.zeros((128, LANES), F32)
        for k in range(FAN):
            hit = lane == spot[:, k:k + 1]
            here = lane128 == line[:, k:k + 1]
            there = lane128 == line[:, k:k + 1] + 4
            for mask, value in ((here, number), (there, weight[:, k:k + 1])):
                total += lax.dot_general(
                    mask.astype(F32).astype(BF16), jnp.where(hit, value, 0.0).astype(BF16),
                    (((0,), (0,)), ((), ())), preferred_element_type=F32,
                )
        tab[o] = total[:32].reshape(4, 8, LANES)

    def first_table(o, step, cc):
        one, _, _ = WAYS[o]
        return remote(
            tab.at[o, (place[one] + step) % 4], tab1.at[o, place[one], core],
            t1s.at[o, step, cc], t1r.at[o, step, cc], moved(place, one, step), (core + cc) % 2,
        )

    for o in range(3):
        one, _, _ = WAYS[o]
        for step in (1, 3, 2, 0):
            for cc in range(2):
                if step or cc:
                    first_table(o, step, cc).start()
        tab1[o, place[one], core] = tab[o, place[one]]

    def second(o, step, back):
        one, two, _ = WAYS[o]
        piece = gs[o].at[place[two], (place[one] + 4 - back) % 4]
        return remote(piece, piece, s2s.at[o, step, back], s2r.at[o, step, back], moved(place, two, step), core)

    def second_table(o, step):
        two = WAYS[o][1]
        return remote(
            tab2s.at[o, (place[two] + step) % 4], tab2.at[o, place[two]],
            t2s.at[o, step], t2r.at[o, step], moved(place, two, step), core,
        )

    def first_wait(o, step, cc):
        one, two, _ = WAYS[o]
        came = gs[o].at[place[two], (place[one] + 4 - step) % 4, (core + cc) % 2]
        remote(came, came, s1s.at[o, step, cc], s1r.at[o, step, cc], place, core).wait_recv()

    def first_table_wait(o, step, cc):
        one, _, _ = WAYS[o]
        came = tab1.at[o, (place[one] + 4 - step) % 4, (core + cc) % 2]
        remote(came, came, t1s.at[o, step, cc], t1r.at[o, step, cc], place, core).wait_recv()

    for back in (0, 1, 3, 2):
        for o in range(3):
            for cc in range(2):
                if back or cc:
                    first_wait(o, back, cc)
            for step in (1, 3, 2):
                second(o, step, back).start()
    for o in range(3):
        for step in (0, 1, 3, 2):
            for cc in range(2):
                if step or cc:
                    first_table_wait(o, step, cc)
        for line in range(4):
            for a in range(4):
                tab2s[o, line, a:a + 1] = tab1[o, a, 0, line:line + 1] + tab1[o, a, 1, line:line + 1]
                tab2s[o, line, 4 + a:5 + a] = tab1[o, a, 0, 4 + line:5 + line] + tab1[o, a, 1, 4 + line:5 + line]
        for step in (1, 3, 2):
            second_table(o, step).start()
        two = WAYS[o][1]
        tab2[o, place[two]] = tab2s[o, place[two]]

    def landing(o, frm, group):
        if o == 0:
            return lambda h: xs[0].at[h, frm, group]
        if o == 1:
            return lambda h: xs[1].at[h, :, frm, group]
        return lambda h: xs[2].at[h, group, :, frm]

    def third(o, step, cc, n, group):
        three = WAYS[o][2]
        to = (place[three] + step) % 4
        c = (core + cc) % 2
        src = rs[o].at[to * 2 + c, group]
        dst = landing(o, place[three], group)(core)
        if step == 0 and cc == 0:
            return pltpu.make_async_copy(src, dst, s3r.at[o, 0, 0, n])
        return remote(src, dst, s3s.at[o, step, cc, n], s3r.at[o, step, cc, n], moved(place, three, step), c)

    def group_of(o, n):
        two = WAYS[o][1]
        gap = n ^ (n >> 1)
        return gap, (place[two] + 4 - gap) % 4

    token_lane = lax.broadcasted_iota(jnp.int32, (ROWS, 2 * TOK), 1).astype(F32) + 1.0

    def pack(n, _):
        for o in range(3):
            one, two, three = WAYS[o]
            gap, group = group_of(o, n)

            @pl.when(n > 0)
            def _():
                for back in range(4):
                    came = gs[o].at[group, (place[one] + 4 - back) % 4]
                    remote(came, came, s2s.at[o, gap, back], s2r.at[o, gap, back], place, core).wait_recv()
                came = tab2.at[o, group]
                remote(came, came, t2s.at[o, gap], t2r.at[o, gap], place, core).wait_recv()

            column = tab2[o, group].T
            for a in range(4):
                pick = jnp.where(column[:ROWS, a:a + 1] == token_lane, 1.0, 0.0).astype(BF16)
                rows = jnp.dot(pick, gs[o][group, a].reshape(2 * TOK, WIDTH[o]), preferred_element_type=F32)
                rs[o][:, group, a] = rows.astype(BF16).reshape(8, PAIR, WIDTH[o])
            for step in (1, 3, 2, 0):
                for cc in range(2):
                    third(o, step, cc, n, group).start()
        return 0

    lax.fori_loop(0, 4, pack, 0)

    for o in range(3):
        for step in range(4):
            for cc in range(2):
                if step or cc:
                    first(o, step, cc).wait_send()
                    first_table(o, step, cc).wait_send()
            if step:
                second_table(o, step).wait_send()
                for back in range(4):
                    second(o, step, back).wait_send()

    for cp in loads:
        cp.wait()

    def arrive(n, _):
        for o in range(3):
            three = WAYS[o][2]
            gap, group = group_of(o, n)
            for step in range(4):
                for cc in range(2):
                    came = landing(o, (place[three] + 4 - step) % 4, group)((core + cc) % 2)
                    if step == 0 and cc == 0:
                        third(o, 0, 0, n, group).wait()
                    else:
                        remote(came, came, s3s.at[o, step, cc, n], s3r.at[o, step, cc, n], place, core).wait_recv()
                        third(o, step, cc, n, group).wait_send()
        return 0

    lax.fori_loop(0, 4, arrive, 0)

    for o in range(3):
        for step in range(4):
            for cc in range(2):
                if step or cc:
                    pl.semaphore_signal(
                        free, inc=1, device_id=device(moved(place, WAYS[o][2], step), (core + cc) % 2), device_id_type=MESH
                    )

    mx, my, mz = place

    def send_a(s, x, q, cc, local):
        h = (core + cc) % 2
        src = xs[0].at[h, x, pl.ds(2 * q, 2)]
        dst = rs[0].at[mx * 2 + core, pl.ds(2 * q, 2)]
        if local:
            return pltpu.make_async_copy(src, dst, rar.at[s, cc])
        return remote(src, dst, ras.at[s, cc], rar.at[s, cc], (x, my, mz), h)

    def send_b(s, x, q, i, cc, local):
        h = (core + cc) % 2
        y = 2 * q + (my + i) % 2
        src = xs[1].at[h, x, y]
        dst = rs[1].at[my * 2 + core, :, x]
        if local:
            return pltpu.make_async_copy(src, dst, rbr.at[s, i, cc])
        return remote(src, dst, rbs.at[s, i, cc], rbr.at[s, i, cc], (mx, y, mz), h)

    def send_c(s, x, q, step, cc):
        h = (core + cc) % 2
        z = (mz + step) % 4
        src = xs[2].at[h, x, pl.ds(2 * q, 2), z]
        dst = rs[2].at[mz * 2 + core, x, pl.ds(2 * q, 2)]
        if step == 0 and cc == 0:
            return pltpu.make_async_copy(src, dst, rcr.at[s, 0, 0])
        return remote(src, dst, rcs.at[s, step, cc], rcr.at[s, step, cc], (mx, my, z), h)

    def block_of(s):
        return (mx + 1 + s // 2) % 4, (my // 2 + s) % 2

    def each(s, act_local, act_remote):
        x, q = block_of(s)
        for cc in range(2):
            if cc:
                act_remote(send_a(s, x, q, cc, False))
            else:
                @pl.when(s < 6)
                def _():
                    act_remote(send_a(s, x, q, 0, False))

                @pl.when(s >= 6)
                def _():
                    act_local(send_a(s, x, q, 0, True))
            for i in range(2):
                if cc or i:
                    act_remote(send_b(s, x, q, i, cc, False))
                else:
                    @pl.when(s % 2 == 1)
                    def _():
                        act_remote(send_b(s, x, q, 0, 0, False))

                    @pl.when(s % 2 == 0)
                    def _():
                        act_local(send_b(s, x, q, 0, 0, True))
            for step in (1, 3, 2, 0):
                if step == 0 and cc == 0:
                    act_local(send_c(s, x, q, 0, 0))
                else:
                    act_remote(send_c(s, x, q, step, cc))

    def expert(s, _):
        x, q = block_of(s)
        pair = pl.ds(2 * q, 2)
        parts = [xs[o][h, x, pair].reshape(ROWS, WIDTH[o]) for h in range(2) for o in range(3)]
        rows = jnp.concatenate(parts, axis=1)
        for f in range(0, FF, 256):
            gate = jnp.dot(rows, wg[:, f:f + 256], preferred_element_type=F32)
            up = jnp.dot(rows, wu[:, f:f + 256], preferred_element_type=F32)
            hidden[:, f:f + 256] = (gate / (1.0 + jnp.exp(-gate)) * up).astype(BF16)
        for h in range(2):
            for o in range(3):
                lo = h * HALF + START[o]
                res = jnp.dot(hidden[...], wd[:, lo:lo + WIDTH[o]], preferred_element_type=F32)
                xs[o][h, x, pair] = res.astype(BF16).reshape(2, 4, PAIR, WIDTH[o])

        @pl.when(s == 0)
        def _():
            pl.semaphore_wait(free, 21)

        each(s, lambda cp: cp.start(), lambda cp: cp.start())
        return 0

    lax.fori_loop(0, 8, expert, 0)

    def returned(s, _):
        each(s, lambda cp: cp.wait(), lambda cp: cp.wait())
        return 0

    lax.fori_loop(0, 8, returned, 0)

    token_row = lax.broadcasted_iota(jnp.int32, (2 * TOK, ROWS), 0).astype(F32) + 1.0

    def reduce_second(o, step):
        two = WAYS[o][1]
        return remote(
            gs[o].at[(place[two] + step) % 4], acc2[o].at[step - 1],
            q2s.at[o, step], q2r.at[o, step], moved(place, two, step), core,
        )

    for step in (1, 3, 2, 0):
        for o in range(3):
            two = WAYS[o][1]
            group = (place[two] + step) % 4
            for a in range(4):
                index = tab2[o, group, a:a + 1, :ROWS]
                w = tab2[o, group, 4 + a:5 + a, :ROWS]
                mix = jnp.where(index == token_row, w, 0.0).astype(BF16)
                part = jnp.dot(mix, rs[o][:, group, a].reshape(ROWS, WIDTH[o]), preferred_element_type=F32)
                gs[o][group, a] = part.astype(BF16).reshape(2, TOK, WIDTH[o])
            if step:
                reduce_second(o, step).start()

    def reduce_first(o, step, cc):
        one, two, _ = WAYS[o]
        c = (core + cc) % 2
        return remote(
            gs[o].at[place[two], (place[one] + step) % 4, c], acc1[o].at[step, cc],
            q1s.at[o, step, cc], q1r.at[o, step, cc], moved(place, one, step), c,
        )

    for o in range(3):
        one, two, _ = WAYS[o]
        for step in (1, 2, 3):
            reduce_second(o, step).wait()
        for step in (1, 3, 2, 0):
            a = (place[one] + step) % 4
            total = gs[o][place[two], a].astype(F32)
            for n in range(3):
                total += acc2[o][n, a].astype(F32)
            gs[o][place[two], a] = total.astype(BF16)
            for cc in range(2):
                if step or cc:
                    reduce_first(o, step, cc).start()
        acc1[o][0, 0] = gs[o][place[two], place[one], core]

    for o in range(3):
        for step in range(4):
            for cc in range(2):
                if step or cc:
                    reduce_first(o, step, cc).wait()
        for cc in range(2):
            h = (core + cc) % 2
            where = pl.ds(pl.multiple_of(h * HALF + START[o], 128), WIDTH[o])
            total = acc1[o][0, cc].astype(F32)
            for step in (1, 2, 3):
                total += acc1[o][step, cc].astype(F32)
            out[:, where] = (resid[:, where].astype(F32) + total).astype(BF16)


def per_device(resid, norm_gain, w_gate, w_up, w_down, route_ids, route_slots, route_weights):
    vmem = pl.BlockSpec(memory_space=pltpu.VMEM)
    hbm = pl.BlockSpec(memory_space=pl.ANY)

    def per_way(*lead, rows):
        return [pltpu.VMEM((*lead, rows, w), BF16) for w in WIDTH]

    dma = pltpu.SemaphoreType.DMA
    return pl.pallas_call(
        kernel,
        out_shape=jax.ShapeDtypeStruct((TOK, D), BF16),
        in_specs=[vmem] * 5 + [hbm] * 3,
        out_specs=vmem,
        scratch_shapes=[
            *per_way(2, rows=TOK),
            *per_way(4, 4, 2, rows=TOK),
            *per_way(8, 4, 4, rows=PAIR),
            *per_way(2, 4, 4, 4, rows=PAIR),
            *per_way(3, 4, 2, rows=TOK),
            *per_way(4, 2, rows=TOK),
            pltpu.VMEM((3, 4, 8, LANES), F32),
            pltpu.VMEM((3, 4, 2, 8, LANES), F32),
            pltpu.VMEM((3, 4, 8, LANES), F32),
            pltpu.VMEM((3, 4, 8, LANES), F32),
            pltpu.VMEM((ROWS, FF), BF16),
            pltpu.VMEM((D, FF), BF16),
            pltpu.VMEM((D, FF), BF16),
            pltpu.VMEM((FF, D), BF16),
            dma((3,)),
            dma((3, 4, 2)), dma((3, 4, 2)), dma((3, 4, 2)), dma((3, 4, 2)),
            dma((3, 4, 4)), dma((3, 4, 4)), dma((3, 4)), dma((3, 4)),
            dma((3, 4, 2, 4)), dma((3, 4, 2, 4)),
            dma((8, 2)), dma((8, 2)),
            dma((8, 2, 2)), dma((8, 2, 2)),
            dma((8, 4, 2)), dma((8, 4, 2)),
            dma((3, 4)), dma((3, 4)),
            dma((3, 4, 2)), dma((3, 4, 2)),
            pltpu.SemaphoreType.REGULAR,
        ],
        compiler_params=pltpu.CompilerParams(
            collective_id=0, has_side_effects=True, vmem_limit_bytes=62 * 2**20
        ),
        cost_estimate=pl.CostEstimate(flops=30 * 10**9, bytes_accessed=11 * 10**6, transcendentals=2 * 10**6),
    )(resid, norm_gain[None, :], route_ids, route_slots, route_weights, w_gate[0], w_up[0], w_down[0])


def solution(mesh):
    rows = P(("dp", "expert"), None)
    expert = P(("dp", "expert"), None, None)
    return jax.shard_map(
        per_device, mesh=mesh, in_specs=(rows, P(), expert, expert, expert, rows, rows, rows), out_specs=rows, check_vma=False
    )
```

```python
import jax
import jax.numpy as jnp
from jax import lax
from jax.experimental import pallas as pl
from jax.experimental.pallas import tpu as pltpu
from jax.sharding import PartitionSpec as P

MESH = pl.DeviceIdType.MESH
F32 = jnp.float32
BF16 = jnp.bfloat16
epsilon = 1e-06

TOK = 128
D = 2048
FF = 768
FAN = 8
CAP = 20
PAIR = 2 * CAP
WAYS = ((2, 1, 0), (0, 2, 1), (1, 0, 2))
WIDTH = (384, 384, 256)
START = (0, 384, 768)
HALF = 1024
LANES = 384
ROWS = 8 * PAIR


def my_place():
    dp = lax.axis_index("dp")
    ex = lax.axis_index("expert")
    return [(dp % 2) * 2 + ex // 2, (dp // 2) % 4, dp // 8], ex % 2


def device(place, core):
    x, y, z = place
    return (z * 8 + y * 2 + x // 2, (x % 2) * 2 + core)


def moved(place, axis, step):
    place = list(place)
    place[axis] = (place[axis] + step) % 4
    return place


def kernel(resid, gain, ids, slots, wts, wg_hbm, wu_hbm, wd_hbm, out,
           tok0, tok1, tok2, g0, g1, g2, r0, r1, r2, x0, x1, x2, a0, a1_, a2_, b0, b1, b2,
           tab, tab1, tab2s, tab2, hidden, wg, wu, wd,
           sem_w, s1s, s1r, t1s, t1r, s2s, s2r, t2s, t2r, s3s, s3r, ras, rar, rbs, rbr, rcs, rcr, q2s, q2r, q1s, q1r, free):
    place, core = my_place()
    toks, gs, rs, xs = (tok0, tok1, tok2), (g0, g1, g2), (r0, r1, r2), (x0, x1, x2)
    acc2, acc1 = (a0, a1_, a2_), (b0, b1, b2)

    def remote(src, dst, ssem, rsem, where, c):
        return pltpu.make_async_remote_copy(
            src_ref=src, dst_ref=dst, send_sem=ssem, recv_sem=rsem,
            device_id=device(where, c), device_id_type=MESH,
        )

    loads = [pltpu.make_async_copy(h, v, sem_w.at[i]) for i, (h, v) in enumerate(((wg_hbm, wg), (wu_hbm, wu), (wd_hbm, wd)))]
    for cp in loads:
        cp.start()

    barrier = pltpu.get_barrier_semaphore()
    for axis in range(3):
        for step in (1, 2, 3):
            for c in range(2):
                pl.semaphore_signal(barrier, inc=1, device_id=device(moved(place, axis, step), c), device_id_type=MESH)
    pl.semaphore_signal(barrier, inc=1, device_id=device(place, 1 - core), device_id_type=MESH)

    floats = resid[...].astype(F32)
    mean_square = jnp.mean(floats * floats, axis=1, keepdims=True)
    normed = (floats * lax.rsqrt(mean_square + epsilon) * gain[...]).astype(BF16)
    for o in range(3):
        for h in range(2):
            lo = h * HALF + START[o]
            toks[o][h] = normed[:, lo:lo + WIDTH[o]]

    pl.semaphore_wait(barrier, 19)

    def first(o, step, cc):
        one, two, _ = WAYS[o]
        h = (core + cc) % 2
        return remote(
            toks[o].at[h], gs[o].at[place[two], place[one], core],
            s1s.at[o, step, cc], s1r.at[o, step, cc], moved(place, one, step), h,
        )

    for step in (1, 3, 2, 0):
        for o in range(3):
            for cc in range(2):
                if step or cc:
                    first(o, step, cc).start()
    for o in range(3):
        one, two, _ = WAYS[o]
        gs[o][place[two], place[one], core] = toks[o][core]

    e = ids[...]
    coords = ((e >> 1) & 3, (e >> 3) & 3, e >> 5)
    sl = slots[...]
    lane = lax.broadcasted_iota(jnp.int32, (TOK, LANES), 1).astype(F32)
    level = lax.broadcasted_iota(jnp.int32, (32, TOK), 0)
    number = (lax.broadcasted_iota(jnp.int32, (TOK, 1), 0) + 1 + core * TOK).astype(F32)
    weight = wts[...].T
    for o in range(3):
        one, two, three = WAYS[o]
        spot = jnp.where(sl >= 0, ((coords[three] * 2 + (e & 1)) * 2 + core) * CAP + sl, -1).astype(F32).T
        line = coords[one] * 8 + coords[two]
        total = jnp.zeros((32, LANES), F32)
        for k in range(FAN):
            hit = lane == spot[:, k:k + 1]
            here = level == line[k:k + 1]
            there = level == line[k:k + 1] + 4
            for mask, value in ((here, number), (there, weight[:, k:k + 1])):
                total += jnp.dot(
                    mask.astype(F32).astype(BF16), jnp.where(hit, value, 0.0).astype(BF16), preferred_element_type=F32
                )
        tab[o] = total.reshape(4, 8, LANES)

    def first_table(o, step, cc):
        one, _, _ = WAYS[o]
        return remote(
            tab.at[o, (place[one] + step) % 4], tab1.at[o, place[one], core],
            t1s.at[o, step, cc], t1r.at[o, step, cc], moved(place, one, step), (core + cc) % 2,
        )

    for o in range(3):
        one, _, _ = WAYS[o]
        for step in (1, 3, 2, 0):
            for cc in range(2):
                if step or cc:
                    first_table(o, step, cc).start()
        tab1[o, place[one], core] = tab[o, place[one]]

    def second(o, step, back):
        one, two, _ = WAYS[o]
        piece = gs[o].at[place[two], (place[one] + 4 - back) % 4]
        return remote(piece, piece, s2s.at[o, step, back], s2r.at[o, step, back], moved(place, two, step), core)

    def forward(o, up, back):
        one, two, _ = WAYS[o]
        piece = gs[o].at[(place[two] + (3 if up else 1)) % 4, (place[one] + 4 - back) % 4, 0 if up else 1]
        at = 0 if up else 2
        return remote(piece, piece, s2s.at[o, at, back], s2r.at[o, at, back], moved(place, two, 1 if up else 3), core)

    def second_wait(o, step, back):
        one, two, _ = WAYS[o]
        came = gs[o].at[(place[two] + 4 - step) % 4, (place[one] + 4 - back) % 4]
        remote(came, came, s2s.at[o, step, back], s2r.at[o, step, back], place, core).wait_recv()

    def forward_wait(o, up, back):
        one, two, _ = WAYS[o]
        at = 0 if up else 2
        came = gs[o].at[(place[two] + 2) % 4, (place[one] + 4 - back) % 4, 0 if up else 1]
        remote(came, came, s2s.at[o, at, back], s2r.at[o, at, back], place, core).wait_recv()

    def second_table(o, step):
        two = WAYS[o][1]
        return remote(
            tab2s.at[o, (place[two] + step) % 4], tab2.at[o, place[two]],
            t2s.at[o, step], t2r.at[o, step], moved(place, two, step), core,
        )

    def first_wait(o, step, cc):
        one, two, _ = WAYS[o]
        came = gs[o].at[place[two], (place[one] + 4 - step) % 4, (core + cc) % 2]
        remote(came, came, s1s.at[o, step, cc], s1r.at[o, step, cc], place, core).wait_recv()

    def first_table_wait(o, step, cc):
        one, _, _ = WAYS[o]
        came = tab1.at[o, (place[one] + 4 - step) % 4, (core + cc) % 2]
        remote(came, came, t1s.at[o, step, cc], t1r.at[o, step, cc], place, core).wait_recv()

    for back in (0, 1, 3, 2):
        for o in range(3):
            for cc in range(2):
                if back or cc:
                    first_wait(o, back, cc)
            for step in (1, 3):
                second(o, step, back).start()
    for o in range(3):
        for step in (0, 1, 3, 2):
            for cc in range(2):
                if step or cc:
                    first_table_wait(o, step, cc)
        for line in range(4):
            for a in range(4):
                tab2s[o, line, a:a + 1] = tab1[o, a, 0, line:line + 1] + tab1[o, a, 1, line:line + 1]
                tab2s[o, line, 4 + a:5 + a] = tab1[o, a, 0, 4 + line:5 + line] + tab1[o, a, 1, 4 + line:5 + line]
        for step in (1, 3, 2):
            second_table(o, step).start()
        two = WAYS[o][1]
        tab2[o, place[two]] = tab2s[o, place[two]]

    def landing(o, frm, group):
        if o == 0:
            return lambda h: xs[0].at[h, frm, group]
        if o == 1:
            return lambda h: xs[1].at[h, :, frm, group]
        return lambda h: xs[2].at[h, group, :, frm]

    def third(o, step, cc, n, group):
        three = WAYS[o][2]
        to = (place[three] + step) % 4
        c = (core + cc) % 2
        src = rs[o].at[to * 2 + c, group]
        dst = landing(o, place[three], group)(core)
        if step == 0 and cc == 0:
            return pltpu.make_async_copy(src, dst, s3r.at[o, 0, 0, n])
        return remote(src, dst, s3s.at[o, step, cc, n], s3r.at[o, step, cc, n], moved(place, three, step), c)

    def group_of(o, n):
        two = WAYS[o][1]
        gap = n ^ (n >> 1)
        return gap, (place[two] + 4 - gap) % 4

    token_lane = lax.broadcasted_iota(jnp.int32, (ROWS, 2 * TOK), 1).astype(F32) + 1.0

    def pack(o, n):
        three = WAYS[o][2]
        gap, group = group_of(o, n)
        column = tab2[o, group].T
        for a in range(4):
            pick = jnp.where(column[:ROWS, a:a + 1] == token_lane, 1.0, 0.0).astype(BF16)
            rows = jnp.dot(pick, gs[o][group, a].reshape(2 * TOK, WIDTH[o]), preferred_element_type=F32)
            rs[o][:, group, a] = rows.astype(BF16).reshape(8, PAIR, WIDTH[o])
        for step in (1, 3, 2, 0):
            for cc in range(2):
                third(o, step, cc, n, group).start()

    for o in range(3):
        pack(o, 0)
    for back in (0, 1, 3, 2):
        for o in range(3):
            for step in (1, 3):
                second_wait(o, step, back)
                forward(o, step == 1, back).start()

    def others(n, _):
        for o in range(3):
            gap, group = group_of(o, n)

            @pl.when(n == 3)
            def _():
                for back in range(4):
                    forward_wait(o, True, back)
                    forward_wait(o, False, back)

            came = tab2.at[o, group]
            remote(came, came, t2s.at[o, gap], t2r.at[o, gap], place, core).wait_recv()
            pack(o, n)
        return 0

    lax.fori_loop(1, 4, others, 0)

    for o in range(3):
        for step in range(4):
            for cc in range(2):
                if step or cc:
                    first(o, step, cc).wait_send()
                    first_table(o, step, cc).wait_send()
            if step:
                second_table(o, step).wait_send()
        for back in range(4):
            for step in (1, 3):
                second(o, step, back).wait_send()
                forward(o, step == 1, back).wait_send()

    for cp in loads:
        cp.wait()

    def arrive(n, _):
        for o in range(3):
            three = WAYS[o][2]
            gap, group = group_of(o, n)
            for step in range(4):
                for cc in range(2):
                    came = landing(o, (place[three] + 4 - step) % 4, group)((core + cc) % 2)
                    if step == 0 and cc == 0:
                        third(o, 0, 0, n, group).wait()
                    else:
                        remote(came, came, s3s.at[o, step, cc, n], s3r.at[o, step, cc, n], place, core).wait_recv()
                        third(o, step, cc, n, group).wait_send()
        return 0

    lax.fori_loop(0, 4, arrive, 0)

    for o in range(3):
        for step in range(4):
            for cc in range(2):
                if step or cc:
                    pl.semaphore_signal(
                        free, inc=1, device_id=device(moved(place, WAYS[o][2], step), (core + cc) % 2), device_id_type=MESH
                    )

    mx, my, mz = place

    def send_a(s, x, q, cc, local):
        h = (core + cc) % 2
        src = xs[0].at[h, x, pl.ds(2 * q, 2)]
        dst = rs[0].at[mx * 2 + core, pl.ds(2 * q, 2)]
        if local:
            return pltpu.make_async_copy(src, dst, rar.at[s, cc])
        return remote(src, dst, ras.at[s, cc], rar.at[s, cc], (x, my, mz), h)

    def send_b(s, x, q, i, cc, local):
        h = (core + cc) % 2
        y = 2 * q + (my + i) % 2
        src = xs[1].at[h, x, y]
        dst = rs[1].at[my * 2 + core, :, x]
        if local:
            return pltpu.make_async_copy(src, dst, rbr.at[s, i, cc])
        return remote(src, dst, rbs.at[s, i, cc], rbr.at[s, i, cc], (mx, y, mz), h)

    def send_c(s, x, q, step, cc):
        h = (core + cc) % 2
        z = (mz + step) % 4
        src = xs[2].at[h, x, pl.ds(2 * q, 2), z]
        dst = rs[2].at[mz * 2 + core, x, pl.ds(2 * q, 2)]
        if step == 0 and cc == 0:
            return pltpu.make_async_copy(src, dst, rcr.at[s, 0, 0])
        return remote(src, dst, rcs.at[s, step, cc], rcr.at[s, step, cc], (mx, my, z), h)

    def block_of(s):
        turn = (s + 1) % 4
        return (mx + (turn ^ (turn >> 1))) % 4, (my // 2 + 1 - s // 4) % 2

    def each(s, act_local, act_remote):
        x, q = block_of(s)
        for cc in range(2):
            if cc:
                act_remote(send_a(s, x, q, cc, False))
            else:
                @pl.when(s % 4 < 3)
                def _():
                    act_remote(send_a(s, x, q, 0, False))

                @pl.when(s % 4 == 3)
                def _():
                    act_local(send_a(s, x, q, 0, True))
            for i in range(2):
                if cc or i:
                    act_remote(send_b(s, x, q, i, cc, False))
                else:
                    @pl.when(s < 4)
                    def _():
                        act_remote(send_b(s, x, q, 0, 0, False))

                    @pl.when(s >= 4)
                    def _():
                        act_local(send_b(s, x, q, 0, 0, True))
            for step in (1, 3, 2, 0):
                if step == 0 and cc == 0:
                    act_local(send_c(s, x, q, 0, 0))
                else:
                    act_remote(send_c(s, x, q, step, cc))

    def expert(s, _):
        x, q = block_of(s)
        pair = pl.ds(2 * q, 2)
        parts = [xs[o][h, x, pair].reshape(ROWS, WIDTH[o]) for h in range(2) for o in range(3)]
        rows = jnp.concatenate(parts, axis=1)
        for f in range(0, FF, 256):
            gate = jnp.dot(rows, wg[:, f:f + 256], preferred_element_type=F32)
            up = jnp.dot(rows, wu[:, f:f + 256], preferred_element_type=F32)
            hidden[:, f:f + 256] = (gate / (1.0 + jnp.exp(-gate)) * up).astype(BF16)
        for h in range(2):
            for o in range(3):
                lo = h * HALF + START[o]
                res = jnp.dot(hidden[...], wd[:, lo:lo + WIDTH[o]], preferred_element_type=F32)
                xs[o][h, x, pair] = res.astype(BF16).reshape(2, 4, PAIR, WIDTH[o])

        @pl.when(s == 0)
        def _():
            pl.semaphore_wait(free, 21)

        each(s, lambda cp: cp.start(), lambda cp: cp.start())
        return 0

    lax.fori_loop(0, 8, expert, 0)

    def returned(s, _):
        each(s, lambda cp: cp.wait(), lambda cp: cp.wait())
        return 0

    lax.fori_loop(0, 8, returned, 0)

    token_row = lax.broadcasted_iota(jnp.int32, (2 * TOK, ROWS), 0).astype(F32) + 1.0

    def reduce_second(o, step):
        two = WAYS[o][1]
        return remote(
            gs[o].at[(place[two] + step) % 4], acc2[o].at[step // 2],
            q2s.at[o, step], q2r.at[o, step], moved(place, two, step), core,
        )

    def reduce_far(o, up):
        two = WAYS[o][1]
        c, at = (0, 0) if up else (1, 2)
        return remote(
            gs[o].at[(place[two] + 2) % 4, :, c], acc2[o].at[2, :, c],
            q2s.at[o, at], q2r.at[o, at], moved(place, two, 1 if up else 3), core,
        )

    for step in (2, 0, 1, 3):
        for o in range(3):
            two = WAYS[o][1]
            group = (place[two] + step) % 4
            if step % 2:
                c = step // 2
                reduce_far(o, step == 1).wait_recv()
            for a in range(4):
                index = tab2[o, group, a:a + 1, :ROWS]
                w = tab2[o, group, 4 + a:5 + a, :ROWS]
                mix = jnp.where(index == token_row, w, 0.0).astype(BF16)
                part = jnp.dot(mix, rs[o][:, group, a].reshape(ROWS, WIDTH[o]), preferred_element_type=F32)
                part = part.reshape(2, TOK, WIDTH[o])
                if step % 2:
                    gs[o][group, a, c] = (part[c] + acc2[o][2, a, c].astype(F32)).astype(BF16)
                    gs[o][group, a, 1 - c] = part[1 - c].astype(BF16)
                else:
                    gs[o][group, a] = part.astype(BF16)
            if step == 2:
                reduce_far(o, True).start()
                reduce_far(o, False).start()
            elif step:
                reduce_second(o, step).start()

    def reduce_first(o, step, cc):
        one, two, _ = WAYS[o]
        c = (core + cc) % 2
        return remote(
            gs[o].at[place[two], (place[one] + step) % 4, c], acc1[o].at[step, cc],
            q1s.at[o, step, cc], q1r.at[o, step, cc], moved(place, one, step), c,
        )

    for o in range(3):
        one, two, _ = WAYS[o]
        for step in (1, 3):
            reduce_second(o, step).wait()
            reduce_far(o, step == 1).wait_send()
        for step in (1, 3, 2, 0):
            a = (place[one] + step) % 4
            total = gs[o][place[two], a].astype(F32)
            for n in range(2):
                total += acc2[o][n, a].astype(F32)
            gs[o][place[two], a] = total.astype(BF16)
            for cc in range(2):
                if step or cc:
                    reduce_first(o, step, cc).start()
        acc1[o][0, 0] = gs[o][place[two], place[one], core]

    for o in range(3):
        for step in range(4):
            for cc in range(2):
                if step or cc:
                    reduce_first(o, step, cc).wait()
        for cc in range(2):
            h = (core + cc) % 2
            where = pl.ds(pl.multiple_of(h * HALF + START[o], 128), WIDTH[o])
            total = acc1[o][0, cc].astype(F32)
            for step in (1, 2, 3):
                total += acc1[o][step, cc].astype(F32)
            out[:, where] = (resid[:, where].astype(F32) + total).astype(BF16)


def per_device(resid, norm_gain, w_gate, w_up, w_down, route_ids, route_slots, route_weights):
    vmem = pl.BlockSpec(memory_space=pltpu.VMEM)
    hbm = pl.BlockSpec(memory_space=pl.ANY)

    def per_way(*lead, rows):
        return [pltpu.VMEM((*lead, rows, w), BF16) for w in WIDTH]

    dma = pltpu.SemaphoreType.DMA
    return pl.pallas_call(
        kernel,
        out_shape=jax.ShapeDtypeStruct((TOK, D), BF16),
        in_specs=[vmem] * 5 + [hbm] * 3,
        out_specs=vmem,
        scratch_shapes=[
            *per_way(2, rows=TOK),
            *per_way(4, 4, 2, rows=TOK),
            *per_way(8, 4, 4, rows=PAIR),
            *per_way(2, 4, 4, 4, rows=PAIR),
            *per_way(3, 4, 2, rows=TOK),
            *per_way(4, 2, rows=TOK),
            pltpu.VMEM((3, 4, 8, LANES), F32),
            pltpu.VMEM((3, 4, 2, 8, LANES), F32),
            pltpu.VMEM((3, 4, 8, LANES), F32),
            pltpu.VMEM((3, 4, 8, LANES), F32),
            pltpu.VMEM((ROWS, FF), BF16),
            pltpu.VMEM((D, FF), BF16),
            pltpu.VMEM((D, FF), BF16),
            pltpu.VMEM((FF, D), BF16),
            dma((3,)),
            dma((3, 4, 2)), dma((3, 4, 2)), dma((3, 4, 2)), dma((3, 4, 2)),
            dma((3, 4, 4)), dma((3, 4, 4)), dma((3, 4)), dma((3, 4)),
            dma((3, 4, 2, 4)), dma((3, 4, 2, 4)),
            dma((8, 2)), dma((8, 2)),
            dma((8, 2, 2)), dma((8, 2, 2)),
            dma((8, 4, 2)), dma((8, 4, 2)),
            dma((3, 4)), dma((3, 4)),
            dma((3, 4, 2)), dma((3, 4, 2)),
            pltpu.SemaphoreType.REGULAR,
        ],
        compiler_params=pltpu.CompilerParams(
            collective_id=0, has_side_effects=True, vmem_limit_bytes=62 * 2**20
        ),
        cost_estimate=pl.CostEstimate(flops=30 * 10**9, bytes_accessed=11 * 10**6, transcendentals=2 * 10**6),
    )(resid, norm_gain[None, :], route_ids.T, route_slots.T, route_weights.T, w_gate[0], w_up[0], w_down[0])


def solution(mesh):
    rows = P(("dp", "expert"), None)
    expert = P(("dp", "expert"), None, None)
    return jax.shard_map(
        per_device, mesh=mesh, in_specs=(rows, P(), expert, expert, expert, rows, rows, rows), out_specs=rows, check_vma=False
    )
```

```python
import functools

import jax
import jax.numpy as jnp
from jax import lax
from jax.experimental import pallas as pl
from jax.experimental.pallas import tpu as pltpu
from jax.sharding import PartitionSpec as P

MESH = pl.DeviceIdType.MESH
F32 = jnp.float32
BF16 = jnp.bfloat16
epsilon = 1e-06

TOK = 128
D = 2048
FF = 768
FAN = 8
CAP = 20
MAIN = 24
OVER = 16
WAYS = ((2, 1, 0), (0, 2, 1), (1, 0, 2))
WIDTH = (384, 384, 256)
START = (0, 384, 768)
HALF = 1024


def my_place():
    dp = lax.axis_index("dp")
    ex = lax.axis_index("expert")
    return [(dp % 2) * 2 + ex // 2, (dp // 2) % 4, dp // 8], ex % 2


def device(place, core):
    x, y, z = place
    return (z * 8 + y * 2 + x // 2, (x % 2) * 2 + core)


def moved(place, axis, step):
    place = list(place)
    place[axis] = (place[axis] + step) % 4
    return place


def kernel(main, over, resid, gain, ids, slots, wts, wg_hbm, wu_hbm, wd_hbm, out, *scratch):
    it = iter(scratch)

    def take(n):
        return tuple(next(it) for _ in range(n))

    toks, gs, rs, xs, acc2, acc1 = (take(3) for _ in range(6))
    tab, tab1, tab2s, tab2, hidden, wg, wu, wd = take(8)
    sem_w, s1s, s1r, t1s, t1r, s2s, s2r, t2s, t2r, s3s, s3r, ras, rar, rbs, rbr, rcs, rcr, q2s, q2r, q1s, q1r, free = take(22)
    if over:
        ro, xo, ys = (take(3) for _ in range(3))
        s3os, s3or, fos, fors, oas, oar, obs, obr, ocs, ocr, yss, ysr = take(12)
    main_slots, over_slots = main // 2, over // 2
    ROWS = 8 * main + 4 * over
    LANES = tab.shape[-1]
    place, core = my_place()

    def remote(src, dst, ssem, rsem, where, c):
        return pltpu.make_async_remote_copy(
            src_ref=src, dst_ref=dst, send_sem=ssem, recv_sem=rsem,
            device_id=device(where, c), device_id_type=MESH,
        )

    loads = [pltpu.make_async_copy(h, v, sem_w.at[i]) for i, (h, v) in enumerate(((wg_hbm, wg), (wu_hbm, wu), (wd_hbm, wd)))]
    for cp in loads:
        cp.start()

    barrier = pltpu.get_barrier_semaphore()
    for axis in range(3):
        for step in (1, 2, 3):
            for c in range(2):
                pl.semaphore_signal(barrier, inc=1, device_id=device(moved(place, axis, step), c), device_id_type=MESH)
    pl.semaphore_signal(barrier, inc=1, device_id=device(place, 1 - core), device_id_type=MESH)

    floats = resid[...].astype(F32)
    mean_square = jnp.mean(floats * floats, axis=1, keepdims=True)
    normed = (floats * lax.rsqrt(mean_square + epsilon) * gain[...]).astype(BF16)
    for o in range(3):
        for h in range(2):
            lo = h * HALF + START[o]
            toks[o][h] = normed[:, lo:lo + WIDTH[o]]

    pl.semaphore_wait(barrier, 19)

    def first(o, step, cc):
        one, two, _ = WAYS[o]
        h = (core + cc) % 2
        return remote(
            toks[o].at[h], gs[o].at[place[two], place[one], core],
            s1s.at[o, step, cc], s1r.at[o, step, cc], moved(place, one, step), h,
        )

    for step in (1, 3, 2, 0):
        for o in range(3):
            for cc in range(2):
                if step or cc:
                    first(o, step, cc).start()
    for o in range(3):
        one, two, _ = WAYS[o]
        gs[o][place[two], place[one], core] = toks[o][core]

    e = ids[...]
    coords = ((e >> 1) & 3, (e >> 3) & 3, e >> 5)
    sl = slots[...]
    lane = lax.broadcasted_iota(jnp.int32, (TOK, LANES), 1).astype(F32)
    level = lax.broadcasted_iota(jnp.int32, (32, TOK), 0)
    number = (lax.broadcasted_iota(jnp.int32, (TOK, 1), 0) + 1 + core * TOK).astype(F32)
    weight = wts[...].T
    for o in range(3):
        one, two, three = WAYS[o]
        spot = ((coords[three] * 2 + (e & 1)) * 2 + core) * main_slots + sl
        if over:
            shared = 8 * main + (coords[three] * 2 + core) * over_slots + sl - main_slots
            spot = jnp.where(sl < main_slots, spot, shared)
        spot = jnp.where(sl >= 0, spot, -1).astype(F32).T
        line = coords[one] * 8 + coords[two]
        total = jnp.zeros((32, LANES), F32)
        for k in range(FAN):
            hit = lane == spot[:, k:k + 1]
            here = level == line[k:k + 1]
            there = level == line[k:k + 1] + 4
            for mask, value in ((here, number), (there, weight[:, k:k + 1])):
                total += jnp.dot(
                    mask.astype(F32).astype(BF16), jnp.where(hit, value, 0.0).astype(BF16), preferred_element_type=F32
                )
        tab[o] = total.reshape(4, 8, LANES)

    def first_table(o, step, cc):
        one, _, _ = WAYS[o]
        return remote(
            tab.at[o, (place[one] + step) % 4], tab1.at[o, place[one], core],
            t1s.at[o, step, cc], t1r.at[o, step, cc], moved(place, one, step), (core + cc) % 2,
        )

    for o in range(3):
        one, _, _ = WAYS[o]
        for step in (1, 3, 2, 0):
            for cc in range(2):
                if step or cc:
                    first_table(o, step, cc).start()
        tab1[o, place[one], core] = tab[o, place[one]]

    def second(o, step, back):
        one, two, _ = WAYS[o]
        piece = gs[o].at[place[two], (place[one] + 4 - back) % 4]
        return remote(piece, piece, s2s.at[o, step, back], s2r.at[o, step, back], moved(place, two, step), core)

    def forward(o, up, back):
        one, two, _ = WAYS[o]
        piece = gs[o].at[(place[two] + (3 if up else 1)) % 4, (place[one] + 4 - back) % 4, 0 if up else 1]
        at = 0 if up else 2
        return remote(piece, piece, s2s.at[o, at, back], s2r.at[o, at, back], moved(place, two, 1 if up else 3), core)

    def second_wait(o, step, back):
        one, two, _ = WAYS[o]
        came = gs[o].at[(place[two] + 4 - step) % 4, (place[one] + 4 - back) % 4]
        remote(came, came, s2s.at[o, step, back], s2r.at[o, step, back], place, core).wait_recv()

    def forward_wait(o, up, back):
        one, two, _ = WAYS[o]
        at = 0 if up else 2
        came = gs[o].at[(place[two] + 2) % 4, (place[one] + 4 - back) % 4, 0 if up else 1]
        remote(came, came, s2s.at[o, at, back], s2r.at[o, at, back], place, core).wait_recv()

    def second_table(o, step):
        two = WAYS[o][1]
        return remote(
            tab2s.at[o, (place[two] + step) % 4], tab2.at[o, place[two]],
            t2s.at[o, step], t2r.at[o, step], moved(place, two, step), core,
        )

    def first_wait(o, step, cc):
        one, two, _ = WAYS[o]
        came = gs[o].at[place[two], (place[one] + 4 - step) % 4, (core + cc) % 2]
        remote(came, came, s1s.at[o, step, cc], s1r.at[o, step, cc], place, core).wait_recv()

    def first_table_wait(o, step, cc):
        one, _, _ = WAYS[o]
        came = tab1.at[o, (place[one] + 4 - step) % 4, (core + cc) % 2]
        remote(came, came, t1s.at[o, step, cc], t1r.at[o, step, cc], place, core).wait_recv()

    for back in (0, 1, 3, 2):
        for o in range(3):
            for cc in range(2):
                if back or cc:
                    first_wait(o, back, cc)
            for step in (1, 3):
                second(o, step, back).start()
    for o in range(3):
        for step in (0, 1, 3, 2):
            for cc in range(2):
                if step or cc:
                    first_table_wait(o, step, cc)
        for line in range(4):
            for a in range(4):
                tab2s[o, line, a:a + 1] = tab1[o, a, 0, line:line + 1] + tab1[o, a, 1, line:line + 1]
                tab2s[o, line, 4 + a:5 + a] = tab1[o, a, 0, 4 + line:5 + line] + tab1[o, a, 1, 4 + line:5 + line]
        for step in (1, 3, 2):
            second_table(o, step).start()
        two = WAYS[o][1]
        tab2[o, place[two]] = tab2s[o, place[two]]

    def landing(o, frm, group, to):
        if o == 0:
            return lambda h: to[0].at[h, frm, group]
        if o == 1:
            return lambda h: to[1].at[h, :, frm, group]
        return lambda h: to[2].at[h, group, :, frm]

    def third(o, step, cc, n, group):
        three = WAYS[o][2]
        to = (place[three] + step) % 4
        c = (core + cc) % 2
        src = rs[o].at[to * 2 + c, group]
        dst = landing(o, place[three], group, xs)(core)
        if step == 0 and cc == 0:
            return pltpu.make_async_copy(src, dst, s3r.at[o, 0, 0, n])
        return remote(src, dst, s3s.at[o, step, cc, n], s3r.at[o, step, cc, n], moved(place, three, step), c)

    def third_over(o, step, n, group):
        three = WAYS[o][2]
        src = ro[o].at[(place[three] + step) % 4, group]
        dst = landing(o, place[three], group, xo)(core)
        if step == 0:
            return pltpu.make_async_copy(src, dst, s3or.at[o, 0, n])
        return remote(src, dst, s3os.at[o, step, n], s3or.at[o, step, n], moved(place, three, step), core)

    def across(o, step, n, group, h):
        came = landing(o, (place[WAYS[o][2]] + 4 - step) % 4, group, xo)(h)
        return remote(came, came, fos.at[o, step, n], fors.at[o, step, n], place, 1 - core)

    def group_of(o, n):
        two = WAYS[o][1]
        gap = n ^ (n >> 1)
        return gap, (place[two] + 4 - gap) % 4

    token_lane = lax.broadcasted_iota(jnp.int32, (ROWS, 2 * TOK), 1).astype(F32) + 1.0

    def pack(o, n):
        three = WAYS[o][2]
        gap, group = group_of(o, n)
        column = tab2[o, group].T
        for a in range(4):
            pick = jnp.where(column[:ROWS, a:a + 1] == token_lane, 1.0, 0.0).astype(BF16)
            rows = jnp.dot(pick, gs[o][group, a].reshape(2 * TOK, WIDTH[o]), preferred_element_type=F32)
            rows = rows.astype(BF16)
            rs[o][:, group, a] = rows[:8 * main].reshape(8, main, WIDTH[o])
            if over:
                ro[o][:, group, a] = rows[8 * main:].reshape(4, over, WIDTH[o])
        for step in (1, 3, 2, 0):
            if over:
                third_over(o, step, n, group).start()
            for cc in range(2):
                third(o, step, cc, n, group).start()

    for o in range(3):
        pack(o, 0)
    for back in (0, 1, 3, 2):
        for o in range(3):
            for step in (1, 3):
                second_wait(o, step, back)
                forward(o, step == 1, back).start()

    def others(n, _):
        for o in range(3):
            gap, group = group_of(o, n)

            @pl.when(n == 3)
            def _():
                for back in range(4):
                    forward_wait(o, True, back)
                    forward_wait(o, False, back)

            came = tab2.at[o, group]
            remote(came, came, t2s.at[o, gap], t2r.at[o, gap], place, core).wait_recv()
            pack(o, n)
        return 0

    lax.fori_loop(1, 4, others, 0)

    for o in range(3):
        for step in range(4):
            for cc in range(2):
                if step or cc:
                    first(o, step, cc).wait_send()
                    first_table(o, step, cc).wait_send()
            if step:
                second_table(o, step).wait_send()
        for back in range(4):
            for step in (1, 3):
                second(o, step, back).wait_send()
                forward(o, step == 1, back).wait_send()

    for cp in loads:
        cp.wait()

    def shared_arrive(n, _):
        for o in range(3):
            gap, group = group_of(o, n)
            for step in range(4):
                if step == 0:
                    third_over(o, 0, n, group).wait()
                else:
                    came = landing(o, (place[WAYS[o][2]] + 4 - step) % 4, group, xo)(core)
                    remote(came, came, s3os.at[o, step, n], s3or.at[o, step, n], place, core).wait_recv()
                    third_over(o, step, n, group).wait_send()
                across(o, step, n, group, core).start()
        return 0

    def arrive(n, _):
        for o in range(3):
            three = WAYS[o][2]
            gap, group = group_of(o, n)
            for step in range(4):
                for cc in range(2):
                    came = landing(o, (place[three] + 4 - step) % 4, group, xs)((core + cc) % 2)
                    if step == 0 and cc == 0:
                        third(o, 0, 0, n, group).wait()
                    else:
                        remote(came, came, s3s.at[o, step, cc, n], s3r.at[o, step, cc, n], place, core).wait_recv()
                        third(o, step, cc, n, group).wait_send()
                if over:
                    across(o, step, n, group, core).wait_send()
                    across(o, step, n, group, 1 - core).wait_recv()
        return 0

    if over:
        lax.fori_loop(0, 4, shared_arrive, 0)
    lax.fori_loop(0, 4, arrive, 0)

    for o in range(3):
        for step in range(4):
            for cc in range(2):
                if step or cc:
                    pl.semaphore_signal(
                        free, inc=1, device_id=device(moved(place, WAYS[o][2], step), (core + cc) % 2), device_id_type=MESH
                    )

    mx, my, mz = place

    def send_a(s, x, q, cc, local):
        h = (core + cc) % 2
        src = xs[0].at[h, x, pl.ds(2 * q, 2)]
        dst = rs[0].at[mx * 2 + core, pl.ds(2 * q, 2)]
        if local:
            return pltpu.make_async_copy(src, dst, rar.at[s, cc])
        return remote(src, dst, ras.at[s, cc], rar.at[s, cc], (x, my, mz), h)

    def send_b(s, x, q, i, cc, local):
        h = (core + cc) % 2
        y = 2 * q + (my + i) % 2
        src = xs[1].at[h, x, y]
        dst = rs[1].at[my * 2 + core, :, x]
        if local:
            return pltpu.make_async_copy(src, dst, rbr.at[s, i, cc])
        return remote(src, dst, rbs.at[s, i, cc], rbr.at[s, i, cc], (mx, y, mz), h)

    def send_c(s, x, q, step, cc):
        h = (core + cc) % 2
        z = (mz + step) % 4
        src = xs[2].at[h, x, pl.ds(2 * q, 2), z]
        dst = rs[2].at[mz * 2 + core, x, pl.ds(2 * q, 2)]
        if step == 0 and cc == 0:
            return pltpu.make_async_copy(src, dst, rcr.at[s, 0, 0])
        return remote(src, dst, rcs.at[s, step, cc], rcr.at[s, step, cc], (mx, my, z), h)

    def over_a(s, x, q, local):
        src, dst = xo[0].at[core, x, pl.ds(2 * q, 2)], ro[0].at[mx, pl.ds(2 * q, 2)]
        if local:
            return pltpu.make_async_copy(src, dst, oar.at[s])
        return remote(src, dst, oas.at[s], oar.at[s], (x, my, mz), core)

    def over_b(s, x, q, i, local):
        y = 2 * q + (my + i) % 2
        src, dst = xo[1].at[core, x, y], ro[1].at[my, :, x]
        if local:
            return pltpu.make_async_copy(src, dst, obr.at[s, i])
        return remote(src, dst, obs.at[s, i], obr.at[s, i], (mx, y, mz), core)

    def over_c(s, x, q, step):
        z = (mz + step) % 4
        src, dst = xo[2].at[core, x, pl.ds(2 * q, 2), z], ro[2].at[mz, x, pl.ds(2 * q, 2)]
        if step == 0:
            return pltpu.make_async_copy(src, dst, ocr.at[s, 0])
        return remote(src, dst, ocs.at[s, step], ocr.at[s, step], (mx, my, z), core)

    def each_over(s, o, act):
        x, q = block_of(s)
        if o == 0:
            @pl.when(s % 4 < 3)
            def _():
                act(over_a(s, x, q, False))

            @pl.when(s % 4 == 3)
            def _():
                act(over_a(s, x, q, True))
        elif o == 1:
            act(over_b(s, x, q, 1, False))

            @pl.when(s < 4)
            def _():
                act(over_b(s, x, q, 0, False))

            @pl.when(s >= 4)
            def _():
                act(over_b(s, x, q, 0, True))
        else:
            for step in (1, 3, 2, 0):
                act(over_c(s, x, q, step))

    def to_sibling(s, o):
        x, q = block_of(s)
        return remote(
            xo[o].at[1 - core, x, pl.ds(2 * q, 2)], ys[o].at[x, pl.ds(2 * q, 2)],
            yss.at[s, o], ysr.at[s, o], place, 1 - core,
        )

    def merge(s):
        x, q = block_of(s)
        pair = pl.ds(2 * q, 2)
        for o in range(3):
            to_sibling(s, o).wait_recv()
            mine = xo[o][core, x, pair].reshape(8 * over, WIDTH[o]).astype(F32)
            theirs = ys[o][x, pair].reshape(8 * over, WIDTH[o]).astype(F32)
            kept = jnp.where(hot > 0.0, mine, theirs).astype(BF16)
            xo[o][core, x, pair] = kept.reshape(2, 4, over, WIDTH[o])
            each_over(s, o, lambda cp: cp.start())

    if over:
        me = ((mz * 4 + my) * 4 + mx) * 2 + core
        filled = jnp.where((ids[...] == me) & (slots[...] >= main_slots), 1.0, 0.0)
        hot = jnp.max(jnp.max(filled, axis=1, keepdims=True), axis=0, keepdims=True)

    def block_of(s):
        turn = (s + 1) % 4
        return (mx + (turn ^ (turn >> 1))) % 4, (my // 2 + 1 - s // 4) % 2

    def each(s, o, act):
        x, q = block_of(s)
        for cc in range(2):
            if o == 0 and cc:
                act(send_a(s, x, q, cc, False))
            elif o == 0:
                @pl.when(s % 4 < 3)
                def _():
                    act(send_a(s, x, q, 0, False))

                @pl.when(s % 4 == 3)
                def _():
                    act(send_a(s, x, q, 0, True))
            elif o == 1:
                for i in range(2):
                    if cc or i:
                        act(send_b(s, x, q, i, cc, False))
                    else:
                        @pl.when(s < 4)
                        def _():
                            act(send_b(s, x, q, 0, 0, False))

                        @pl.when(s >= 4)
                        def _():
                            act(send_b(s, x, q, 0, 0, True))
            else:
                for step in (1, 3, 2, 0):
                    act(send_c(s, x, q, step, cc))

    def expert(s, _):
        x, q = block_of(s)
        pair = pl.ds(2 * q, 2)
        halves = [(h, o) for h in range(2) for o in range(3)]
        rows = jnp.concatenate([xs[o][h, x, pair].reshape(8 * main, WIDTH[o]) for h, o in halves], axis=1)
        if over:
            shared = jnp.concatenate([xo[o][h, x, pair].reshape(8 * over, WIDTH[o]) for h, o in halves], axis=1)
            rows = jnp.concatenate([rows, shared], axis=0)
        for f in range(0, FF, 256):
            gate = jnp.dot(rows, wg[:, f:f + 256], preferred_element_type=F32)
            up = jnp.dot(rows, wu[:, f:f + 256], preferred_element_type=F32)
            hidden[:, f:f + 256] = (gate / (1.0 + jnp.exp(-gate)) * up).astype(BF16)
        for h in range(2):
            for o in range(3):
                lo = h * HALF + START[o]
                res = jnp.dot(hidden[...], wd[:, lo:lo + WIDTH[o]], preferred_element_type=F32)
                res = res.astype(BF16)
                xs[o][h, x, pair] = res[:8 * main].reshape(2, 4, main, WIDTH[o])
                if over:
                    xo[o][h, x, pair] = res[8 * main:].reshape(2, 4, over, WIDTH[o])

        @pl.when(s == 0)
        def _():
            pl.semaphore_wait(free, 21)

        for o in range(3):
            if over:
                to_sibling(s, o).start()
            each(s, o, lambda cp: cp.start())
        if over:
            @pl.when(s > 0)
            def _():
                merge(s - 1)
        return 0

    lax.fori_loop(0, 8, expert, 0)
    if over:
        merge(7)

    def returned(o):
        def one_block(s, _):
            each(s, o, lambda cp: cp.wait())
            if over:
                each_over(s, o, lambda cp: cp.wait())
                to_sibling(s, o).wait_send()
            return 0

        lax.fori_loop(0, 8, one_block, 0)

    token_row = lax.broadcasted_iota(jnp.int32, (2 * TOK, ROWS), 0).astype(F32) + 1.0

    FAR, DIRECT, SUM = range(3)

    def push(o, up, kind, turn):
        one, two, _ = WAYS[o]
        step, c = (1, 0) if up else (3, 1)
        a = (place[one] + turn) % 4
        group = (place[two] + (2 if kind == FAR else step)) % 4
        if kind == DIRECT:
            c = 1 - c
        slot = 2 if kind == FAR else step // 2
        at = kind if up else 3 + kind
        return remote(
            gs[o].at[group, a, c], acc2[o].at[slot, a, c],
            q2s.at[o, at, turn], q2r.at[o, at, turn], moved(place, two, step), core,
        )

    def combine(o, step):
        one, two, _ = WAYS[o]
        group = (place[two] + step) % 4
        for turn in (1, 3, 2, 0):
            a = (place[one] + turn) % 4
            index = tab2[o, group, pl.ds(a, 1), :ROWS]
            w = tab2[o, group, pl.ds(4 + a, 1), :ROWS]
            mix = jnp.where(index == token_row, w, 0.0).astype(BF16)
            rows = rs[o][:, group, a].reshape(8 * main, WIDTH[o])
            if over:
                rows = jnp.concatenate([rows, ro[o][:, group, a].reshape(4 * over, WIDTH[o])], axis=0)
            part = jnp.dot(mix, rows, preferred_element_type=F32)
            gs[o][group, a] = part.astype(BF16).reshape(2, TOK, WIDTH[o])
            if step == 2:
                push(o, True, FAR, turn).start()
                push(o, False, FAR, turn).start()
            elif step:
                push(o, step == 1, DIRECT, turn).start()

    returned(2)
    for step in (2, 1, 3, 0):
        combine(2, step)
    returned(0)
    returned(1)
    for step in (2, 1, 3, 0):
        combine(0, step)
        combine(1, step)

    for turn in (1, 3, 2, 0):
        for o in (2, 0, 1):
            one, two, _ = WAYS[o]
            a = (place[one] + turn) % 4
            for up in (True, False):
                step, c = (1, 0) if up else (3, 1)
                group = (place[two] + step) % 4
                push(o, up, FAR, turn).wait_recv()
                gs[o][group, a, c] = (gs[o][group, a, c].astype(F32) + acc2[o][2, a, c].astype(F32)).astype(BF16)
                push(o, up, SUM, turn).start()

    def reduce_first(o, step, cc):
        one, two, _ = WAYS[o]
        c = (core + cc) % 2
        return remote(
            gs[o].at[place[two], (place[one] + step) % 4, c], acc1[o].at[step, cc],
            q1s.at[o, step, cc], q1r.at[o, step, cc], moved(place, one, step), c,
        )

    for step in (1, 3, 2, 0):
        for o in (2, 0, 1):
            one, two, _ = WAYS[o]
            a = (place[one] + step) % 4
            for up in (True, False):
                push(o, up, FAR, step).wait_send()
                push(o, up, DIRECT, step).wait()
                push(o, up, SUM, step).wait()
            total = gs[o][place[two], a].astype(F32)
            for n in range(2):
                total += acc2[o][n, a].astype(F32)
            gs[o][place[two], a] = total.astype(BF16)
            for cc in range(2):
                if step or cc:
                    reduce_first(o, step, cc).start()
            if step == 0:
                acc1[o][0, 0] = gs[o][place[two], place[one], core]

    for o in (2, 0, 1):
        for step in range(4):
            for cc in range(2):
                if step or cc:
                    reduce_first(o, step, cc).wait()
        for cc in range(2):
            h = (core + cc) % 2
            where = pl.ds(pl.multiple_of(h * HALF + START[o], 128), WIDTH[o])
            total = acc1[o][0, cc].astype(F32)
            for step in (1, 2, 3):
                total += acc1[o][step, cc].astype(F32)
            out[:, where] = (resid[:, where].astype(F32) + total).astype(BF16)


def layer(main, over, number, resid, gain, ids, slots, wts, w_gate, w_up, w_down):
    vmem = pl.BlockSpec(memory_space=pltpu.VMEM)
    hbm = pl.BlockSpec(memory_space=pl.ANY)
    lanes = -(-(8 * main + 4 * over) // 128) * 128

    def per_way(*lead, rows):
        return [pltpu.VMEM((*lead, rows, w), BF16) for w in WIDTH]

    def pairs(*shapes):
        return [pltpu.SemaphoreType.DMA(shape) for shape in shapes for _ in range(2)]

    scratch = [
        *per_way(2, rows=TOK),
        *per_way(4, 4, 2, rows=TOK),
        *per_way(8, 4, 4, rows=main),
        *per_way(2, 4, 4, 4, rows=main),
        *per_way(3, 4, 2, rows=TOK),
        *per_way(4, 2, rows=TOK),
        pltpu.VMEM((3, 4, 8, lanes), F32),
        pltpu.VMEM((3, 4, 2, 8, lanes), F32),
        pltpu.VMEM((3, 4, 8, lanes), F32),
        pltpu.VMEM((3, 4, 8, lanes), F32),
        pltpu.VMEM((8 * (main + over), FF), BF16),
        pltpu.VMEM((D, FF), BF16),
        pltpu.VMEM((D, FF), BF16),
        pltpu.VMEM((FF, D), BF16),
        pltpu.SemaphoreType.DMA((3,)),
        *pairs((3, 4, 2), (3, 4, 2), (3, 4, 4), (3, 4), (3, 4, 2, 4), (8, 2), (8, 2, 2), (8, 4, 2), (3, 6, 4), (3, 4, 2)),
        pltpu.SemaphoreType.REGULAR,
    ]
    if over:
        scratch += [
            *per_way(4, 4, 4, rows=over),
            *per_way(2, 4, 4, 4, rows=over),
            *per_way(4, 4, 4, rows=over),
            *pairs((3, 4, 4), (3, 4, 4), (8,), (8, 2), (8, 4), (8, 3)),
        ]
    return pl.pallas_call(
        functools.partial(kernel, main, over),
        out_shape=jax.ShapeDtypeStruct((TOK, D), BF16),
        in_specs=[vmem] * 5 + [hbm] * 3,
        out_specs=vmem,
        scratch_shapes=scratch,
        compiler_params=pltpu.CompilerParams(
            collective_id=number, has_side_effects=True, vmem_limit_bytes=62 * 2**20
        ),
        cost_estimate=pl.CostEstimate(flops=30 * 10**9, bytes_accessed=11 * 10**6, transcendentals=2 * 10**6),
    )(resid, gain, ids, slots, wts, w_gate, w_up, w_down)


def per_device(resid, norm_gain, w_gate, w_up, w_down, route_ids, route_slots, route_weights):
    ids, slots, wts = route_ids.T, route_slots.T, route_weights.T
    chips = lax.broadcasted_iota(jnp.int32, (64, 1, 1), 0)
    past = slots >= MAIN // 2
    first = jnp.any((ids[None] == 2 * chips) & past[None], axis=(1, 2))
    second = jnp.any((ids[None] == 2 * chips + 1) & past[None], axis=(1, 2))
    return lax.cond(
        jnp.any(first & second),
        functools.partial(layer, 2 * CAP, 0, 1),
        functools.partial(layer, MAIN, OVER, 0),
        resid, norm_gain[None, :], ids, slots, wts, w_gate[0], w_up[0], w_down[0],
    )


def solution(mesh):
    rows = P(("dp", "expert"), None)
    expert = P(("dp", "expert"), None, None)
    return jax.shard_map(
        per_device, mesh=mesh, in_specs=(rows, P(), expert, expert, expert, rows, rows, rows), out_specs=rows, check_vma=False
    )
```

```python
import functools

import jax
import jax.numpy as jnp
from jax import lax
from jax.experimental import pallas as pl
from jax.experimental.pallas import tpu as pltpu
from jax.sharding import PartitionSpec as P

MESH = pl.DeviceIdType.MESH
F32 = jnp.float32
BF16 = jnp.bfloat16
epsilon = 1e-06

TOK = 128
D = 2048
FF = 768
FAN = 8
CAP = 20
MAIN = 24
OVER = 16
WAYS = ((2, 1, 0), (0, 2, 1), (1, 0, 2))
WIDTH = (384, 384, 256)
START = (0, 384, 768)
HALF = 1024


def my_place():
    dp = lax.axis_index("dp")
    ex = lax.axis_index("expert")
    return [(dp % 2) * 2 + ex // 2, (dp // 2) % 4, dp // 8], ex % 2


def device(place, core):
    x, y, z = place
    return (z * 8 + y * 2 + x // 2, (x % 2) * 2 + core)


def moved(place, axis, step):
    place = list(place)
    place[axis] = (place[axis] + step) % 4
    return place


def kernel(main, over, resid, gain, ids, slots, wts, wg_hbm, wu_hbm, wd_hbm, out, *scratch):
    if over:
        flag, *scratch = scratch
    it = iter(scratch)

    def take(n):
        return tuple(next(it) for _ in range(n))

    toks, gs, rs, xs, acc2, acc1 = (take(3) for _ in range(6))
    tab, tab1, tab2s, tab2, hidden, wg, wu, wd = take(8)
    sem_w, s1s, s1r, t1s, t1r, s2s, s2r, t2s, t2r, s3s, s3r, ras, rar, rbs, rbr, rcs, rcr, q2s, q2r, q1s, q1r, free = take(22)
    if over:
        ro, xo, ys = (take(3) for _ in range(3))
        s3os, s3or, fos, fors, oas, oar, obs, obr, ocs, ocr, yss, ysr = take(12)
    main_slots, over_slots = main // 2, over // 2
    ROWS = 8 * main + 4 * over
    LANES = tab.shape[-1]
    place, core = my_place()

    def remote(src, dst, ssem, rsem, where, c):
        return pltpu.make_async_remote_copy(
            src_ref=src, dst_ref=dst, send_sem=ssem, recv_sem=rsem,
            device_id=device(where, c), device_id_type=MESH,
        )

    loads = [pltpu.make_async_copy(h, v, sem_w.at[i]) for i, (h, v) in enumerate(((wg_hbm, wg), (wu_hbm, wu), (wd_hbm, wd)))]
    for cp in loads:
        cp.start()

    barrier = pltpu.get_barrier_semaphore()
    for axis in range(3):
        for step in (1, 2, 3):
            for c in range(2):
                pl.semaphore_signal(barrier, inc=1, device_id=device(moved(place, axis, step), c), device_id_type=MESH)
    pl.semaphore_signal(barrier, inc=1, device_id=device(place, 1 - core), device_id_type=MESH)

    floats = resid[...].astype(F32)
    mean_square = jnp.mean(floats * floats, axis=1, keepdims=True)
    normed = (floats * lax.rsqrt(mean_square + epsilon) * gain[...]).astype(BF16)
    for o in range(3):
        for h in range(2):
            lo = h * HALF + START[o]
            toks[o][h] = normed[:, lo:lo + WIDTH[o]]

    pl.semaphore_wait(barrier, 19)

    def first(o, step, cc):
        one, two, _ = WAYS[o]
        h = (core + cc) % 2
        return remote(
            toks[o].at[h], gs[o].at[place[two], place[one], core],
            s1s.at[o, step, cc], s1r.at[o, step, cc], moved(place, one, step), h,
        )

    for step in (1, 3, 2, 0):
        for o in range(3):
            for cc in range(2):
                if step or cc:
                    first(o, step, cc).start()
    for o in range(3):
        one, two, _ = WAYS[o]
        gs[o][place[two], place[one], core] = toks[o][core]

    e = ids[...]
    coords = ((e >> 1) & 3, (e >> 3) & 3, e >> 5)
    sl = slots[...]
    lane = lax.broadcasted_iota(jnp.int32, (TOK, LANES), 1).astype(F32)
    level = lax.broadcasted_iota(jnp.int32, (32, TOK), 0)
    number = (lax.broadcasted_iota(jnp.int32, (TOK, 1), 0) + 1 + core * TOK).astype(F32)
    weight = wts[...].T
    for o in range(3):
        one, two, three = WAYS[o]
        spot = ((coords[three] * 2 + (e & 1)) * 2 + core) * main_slots + sl
        if over:
            shared = 8 * main + (coords[three] * 2 + core) * over_slots + sl - main_slots
            spot = jnp.where(sl < main_slots, spot, shared)
        spot = jnp.where(sl >= 0, spot, -1).astype(F32).T
        line = coords[one] * 8 + coords[two]
        total = jnp.zeros((32, LANES), F32)
        for k in range(FAN):
            hit = lane == spot[:, k:k + 1]
            here = level == line[k:k + 1]
            there = level == line[k:k + 1] + 4
            for mask, value in ((here, number), (there, weight[:, k:k + 1])):
                total += jnp.dot(
                    mask.astype(F32).astype(BF16), jnp.where(hit, value, 0.0).astype(BF16), preferred_element_type=F32
                )
        tab[o] = total.reshape(4, 8, LANES)

    if over:
        number_e = lax.broadcasted_iota(jnp.int32, (2, 64, TOK), 1) * 2 + lax.broadcasted_iota(jnp.int32, (2, 64, TOK), 0)
        seen = jnp.zeros((2, 64, TOK), F32)
        for k in range(FAN):
            past = (sl[k:k + 1] >= main_slots)[None]
            seen = jnp.where((number_e == e[k:k + 1][None]) & past, 1.0, seen)
        seen = jnp.max(seen, axis=2, keepdims=True)
        flag[...] = jnp.broadcast_to(jnp.max(seen[0] * seen[1], axis=0, keepdims=True), flag.shape)

    def first_table(o, step, cc):
        one, _, _ = WAYS[o]
        return remote(
            tab.at[o, (place[one] + step) % 4], tab1.at[o, place[one], core],
            t1s.at[o, step, cc], t1r.at[o, step, cc], moved(place, one, step), (core + cc) % 2,
        )

    for o in range(3):
        one, _, _ = WAYS[o]
        for step in (1, 3, 2, 0):
            for cc in range(2):
                if step or cc:
                    first_table(o, step, cc).start()
        tab1[o, place[one], core] = tab[o, place[one]]

    def second(o, step, back):
        one, two, _ = WAYS[o]
        piece = gs[o].at[place[two], (place[one] + 4 - back) % 4]
        return remote(piece, piece, s2s.at[o, step, back], s2r.at[o, step, back], moved(place, two, step), core)

    def forward(o, up, back):
        one, two, _ = WAYS[o]
        piece = gs[o].at[(place[two] + (3 if up else 1)) % 4, (place[one] + 4 - back) % 4, 0 if up else 1]
        at = 0 if up else 2
        return remote(piece, piece, s2s.at[o, at, back], s2r.at[o, at, back], moved(place, two, 1 if up else 3), core)

    def second_wait(o, step, back):
        one, two, _ = WAYS[o]
        came = gs[o].at[(place[two] + 4 - step) % 4, (place[one] + 4 - back) % 4]
        remote(came, came, s2s.at[o, step, back], s2r.at[o, step, back], place, core).wait_recv()

    def forward_wait(o, up, back):
        one, two, _ = WAYS[o]
        at = 0 if up else 2
        came = gs[o].at[(place[two] + 2) % 4, (place[one] + 4 - back) % 4, 0 if up else 1]
        remote(came, came, s2s.at[o, at, back], s2r.at[o, at, back], place, core).wait_recv()

    def second_table(o, step):
        two = WAYS[o][1]
        return remote(
            tab2s.at[o, (place[two] + step) % 4], tab2.at[o, place[two]],
            t2s.at[o, step], t2r.at[o, step], moved(place, two, step), core,
        )

    def first_wait(o, step, cc):
        one, two, _ = WAYS[o]
        came = gs[o].at[place[two], (place[one] + 4 - step) % 4, (core + cc) % 2]
        remote(came, came, s1s.at[o, step, cc], s1r.at[o, step, cc], place, core).wait_recv()

    def first_table_wait(o, step, cc):
        one, _, _ = WAYS[o]
        came = tab1.at[o, (place[one] + 4 - step) % 4, (core + cc) % 2]
        remote(came, came, t1s.at[o, step, cc], t1r.at[o, step, cc], place, core).wait_recv()

    for back in (0, 1, 3, 2):
        for o in range(3):
            for cc in range(2):
                if back or cc:
                    first_wait(o, back, cc)
            for step in (1, 3):
                second(o, step, back).start()
    for o in range(3):
        for step in (0, 1, 3, 2):
            for cc in range(2):
                if step or cc:
                    first_table_wait(o, step, cc)
        for line in range(4):
            for a in range(4):
                tab2s[o, line, a:a + 1] = tab1[o, a, 0, line:line + 1] + tab1[o, a, 1, line:line + 1]
                tab2s[o, line, 4 + a:5 + a] = tab1[o, a, 0, 4 + line:5 + line] + tab1[o, a, 1, 4 + line:5 + line]
        for step in (1, 3, 2):
            second_table(o, step).start()
        two = WAYS[o][1]
        tab2[o, place[two]] = tab2s[o, place[two]]

    def landing(o, frm, group, to):
        if o == 0:
            return lambda h: to[0].at[h, frm, group]
        if o == 1:
            return lambda h: to[1].at[h, :, frm, group]
        return lambda h: to[2].at[h, group, :, frm]

    def third(o, step, cc, n, group):
        three = WAYS[o][2]
        to = (place[three] + step) % 4
        c = (core + cc) % 2
        src = rs[o].at[to * 2 + c, group]
        dst = landing(o, place[three], group, xs)(core)
        if step == 0 and cc == 0:
            return pltpu.make_async_copy(src, dst, s3r.at[o, 0, 0, n])
        return remote(src, dst, s3s.at[o, step, cc, n], s3r.at[o, step, cc, n], moved(place, three, step), c)

    def third_over(o, step, n, group):
        three = WAYS[o][2]
        src = ro[o].at[(place[three] + step) % 4, group]
        dst = landing(o, place[three], group, xo)(core)
        if step == 0:
            return pltpu.make_async_copy(src, dst, s3or.at[o, 0, n])
        return remote(src, dst, s3os.at[o, step, n], s3or.at[o, step, n], moved(place, three, step), core)

    def across(o, step, n, group, h):
        came = landing(o, (place[WAYS[o][2]] + 4 - step) % 4, group, xo)(h)
        return remote(came, came, fos.at[o, step, n], fors.at[o, step, n], place, 1 - core)

    def group_of(o, n):
        two = WAYS[o][1]
        gap = n ^ (n >> 1)
        return gap, (place[two] + 4 - gap) % 4

    token_lane = lax.broadcasted_iota(jnp.int32, (ROWS, 2 * TOK), 1).astype(F32) + 1.0

    def pack(o, n):
        three = WAYS[o][2]
        gap, group = group_of(o, n)
        column = tab2[o, group].T
        for a in range(4):
            pick = jnp.where(column[:ROWS, a:a + 1] == token_lane, 1.0, 0.0).astype(BF16)
            rows = jnp.dot(pick, gs[o][group, a].reshape(2 * TOK, WIDTH[o]), preferred_element_type=F32)
            rows = rows.astype(BF16)
            rs[o][:, group, a] = rows[:8 * main].reshape(8, main, WIDTH[o])
            if over:
                ro[o][:, group, a] = rows[8 * main:].reshape(4, over, WIDTH[o])
        for step in (1, 3, 2, 0):
            if over:
                third_over(o, step, n, group).start()
            for cc in range(2):
                third(o, step, cc, n, group).start()

    for o in range(3):
        pack(o, 0)
    for back in (0, 1, 3, 2):
        for o in range(3):
            for step in (1, 3):
                second_wait(o, step, back)
                forward(o, step == 1, back).start()

    def others(n, _):
        for o in range(3):
            gap, group = group_of(o, n)

            @pl.when(n == 3)
            def _():
                for back in range(4):
                    forward_wait(o, True, back)
                    forward_wait(o, False, back)

            came = tab2.at[o, group]
            remote(came, came, t2s.at[o, gap], t2r.at[o, gap], place, core).wait_recv()
            pack(o, n)
        return 0

    lax.fori_loop(1, 4, others, 0)

    for o in range(3):
        for step in range(4):
            for cc in range(2):
                if step or cc:
                    first(o, step, cc).wait_send()
                    first_table(o, step, cc).wait_send()
            if step:
                second_table(o, step).wait_send()
        for back in range(4):
            for step in (1, 3):
                second(o, step, back).wait_send()
                forward(o, step == 1, back).wait_send()

    for cp in loads:
        cp.wait()

    def shared_arrive(n, _):
        for o in range(3):
            gap, group = group_of(o, n)
            for step in range(4):
                if step == 0:
                    third_over(o, 0, n, group).wait()
                else:
                    came = landing(o, (place[WAYS[o][2]] + 4 - step) % 4, group, xo)(core)
                    remote(came, came, s3os.at[o, step, n], s3or.at[o, step, n], place, core).wait_recv()
                    third_over(o, step, n, group).wait_send()
                across(o, step, n, group, core).start()
        return 0

    def arrive(n, _):
        for o in range(3):
            three = WAYS[o][2]
            gap, group = group_of(o, n)
            for step in range(4):
                for cc in range(2):
                    came = landing(o, (place[three] + 4 - step) % 4, group, xs)((core + cc) % 2)
                    if step == 0 and cc == 0:
                        third(o, 0, 0, n, group).wait()
                    else:
                        remote(came, came, s3s.at[o, step, cc, n], s3r.at[o, step, cc, n], place, core).wait_recv()
                        third(o, step, cc, n, group).wait_send()
                if over:
                    across(o, step, n, group, core).wait_send()
                    across(o, step, n, group, 1 - core).wait_recv()
        return 0

    if over:
        lax.fori_loop(0, 4, shared_arrive, 0)
    lax.fori_loop(0, 4, arrive, 0)

    for o in range(3):
        for step in range(4):
            for cc in range(2):
                if step or cc:
                    pl.semaphore_signal(
                        free, inc=1, device_id=device(moved(place, WAYS[o][2], step), (core + cc) % 2), device_id_type=MESH
                    )

    mx, my, mz = place

    def send_a(s, x, q, cc, local):
        h = (core + cc) % 2
        src = xs[0].at[h, x, pl.ds(2 * q, 2)]
        dst = rs[0].at[mx * 2 + core, pl.ds(2 * q, 2)]
        if local:
            return pltpu.make_async_copy(src, dst, rar.at[s, cc])
        return remote(src, dst, ras.at[s, cc], rar.at[s, cc], (x, my, mz), h)

    def send_b(s, x, q, i, cc, local):
        h = (core + cc) % 2
        y = 2 * q + (my + i) % 2
        src = xs[1].at[h, x, y]
        dst = rs[1].at[my * 2 + core, :, x]
        if local:
            return pltpu.make_async_copy(src, dst, rbr.at[s, i, cc])
        return remote(src, dst, rbs.at[s, i, cc], rbr.at[s, i, cc], (mx, y, mz), h)

    def send_c(s, x, q, step, cc):
        h = (core + cc) % 2
        z = (mz + step) % 4
        src = xs[2].at[h, x, pl.ds(2 * q, 2), z]
        dst = rs[2].at[mz * 2 + core, x, pl.ds(2 * q, 2)]
        if step == 0 and cc == 0:
            return pltpu.make_async_copy(src, dst, rcr.at[s, 0, 0])
        return remote(src, dst, rcs.at[s, step, cc], rcr.at[s, step, cc], (mx, my, z), h)

    def over_a(s, x, q, local):
        src, dst = xo[0].at[core, x, pl.ds(2 * q, 2)], ro[0].at[mx, pl.ds(2 * q, 2)]
        if local:
            return pltpu.make_async_copy(src, dst, oar.at[s])
        return remote(src, dst, oas.at[s], oar.at[s], (x, my, mz), core)

    def over_b(s, x, q, i, local):
        y = 2 * q + (my + i) % 2
        src, dst = xo[1].at[core, x, y], ro[1].at[my, :, x]
        if local:
            return pltpu.make_async_copy(src, dst, obr.at[s, i])
        return remote(src, dst, obs.at[s, i], obr.at[s, i], (mx, y, mz), core)

    def over_c(s, x, q, step):
        z = (mz + step) % 4
        src, dst = xo[2].at[core, x, pl.ds(2 * q, 2), z], ro[2].at[mz, x, pl.ds(2 * q, 2)]
        if step == 0:
            return pltpu.make_async_copy(src, dst, ocr.at[s, 0])
        return remote(src, dst, ocs.at[s, step], ocr.at[s, step], (mx, my, z), core)

    def each_over(s, o, act):
        x, q = block_of(s)
        if o == 0:
            @pl.when(s % 4 < 3)
            def _():
                act(over_a(s, x, q, False))

            @pl.when(s % 4 == 3)
            def _():
                act(over_a(s, x, q, True))
        elif o == 1:
            act(over_b(s, x, q, 1, False))

            @pl.when(s < 4)
            def _():
                act(over_b(s, x, q, 0, False))

            @pl.when(s >= 4)
            def _():
                act(over_b(s, x, q, 0, True))
        else:
            for step in (1, 3, 2, 0):
                act(over_c(s, x, q, step))

    def to_sibling(s, o):
        x, q = block_of(s)
        return remote(
            xo[o].at[1 - core, x, pl.ds(2 * q, 2)], ys[o].at[x, pl.ds(2 * q, 2)],
            yss.at[s, o], ysr.at[s, o], place, 1 - core,
        )

    def merge(s):
        x, q = block_of(s)
        pair = pl.ds(2 * q, 2)
        for o in range(3):
            to_sibling(s, o).wait_recv()
            mine = xo[o][core, x, pair].reshape(8 * over, WIDTH[o]).astype(F32)
            theirs = ys[o][x, pair].reshape(8 * over, WIDTH[o]).astype(F32)
            kept = jnp.where(hot > 0.0, mine, theirs).astype(BF16)
            xo[o][core, x, pair] = kept.reshape(2, 4, over, WIDTH[o])
            each_over(s, o, lambda cp: cp.start())

    if over:
        me = ((mz * 4 + my) * 4 + mx) * 2 + core
        filled = jnp.where((ids[...] == me) & (slots[...] >= main_slots), 1.0, 0.0)
        hot = jnp.max(jnp.max(filled, axis=1, keepdims=True), axis=0, keepdims=True)

    def block_of(s):
        turn = (s + 1) % 4
        return (mx + (turn ^ (turn >> 1))) % 4, (my // 2 + 1 - s // 4) % 2

    def each(s, o, act):
        x, q = block_of(s)
        for cc in range(2):
            if o == 0 and cc:
                act(send_a(s, x, q, cc, False))
            elif o == 0:
                @pl.when(s % 4 < 3)
                def _():
                    act(send_a(s, x, q, 0, False))

                @pl.when(s % 4 == 3)
                def _():
                    act(send_a(s, x, q, 0, True))
            elif o == 1:
                for i in range(2):
                    if cc or i:
                        act(send_b(s, x, q, i, cc, False))
                    else:
                        @pl.when(s < 4)
                        def _():
                            act(send_b(s, x, q, 0, 0, False))

                        @pl.when(s >= 4)
                        def _():
                            act(send_b(s, x, q, 0, 0, True))
            else:
                for step in (1, 3, 2, 0):
                    act(send_c(s, x, q, step, cc))

    def expert(s, _):
        x, q = block_of(s)
        pair = pl.ds(2 * q, 2)
        halves = [(h, o) for h in range(2) for o in range(3)]
        rows = jnp.concatenate([xs[o][h, x, pair].reshape(8 * main, WIDTH[o]) for h, o in halves], axis=1)
        if over:
            shared = jnp.concatenate([xo[o][h, x, pair].reshape(8 * over, WIDTH[o]) for h, o in halves], axis=1)
            rows = jnp.concatenate([rows, shared], axis=0)
        for f in range(0, FF, 256):
            gate = jnp.dot(rows, wg[:, f:f + 256], preferred_element_type=F32)
            up = jnp.dot(rows, wu[:, f:f + 256], preferred_element_type=F32)
            hidden[:, f:f + 256] = (gate / (1.0 + jnp.exp(-gate)) * up).astype(BF16)
        for h in range(2):
            for o in range(3):
                lo = h * HALF + START[o]
                res = jnp.dot(hidden[...], wd[:, lo:lo + WIDTH[o]], preferred_element_type=F32)
                res = res.astype(BF16)
                xs[o][h, x, pair] = res[:8 * main].reshape(2, 4, main, WIDTH[o])
                if over:
                    xo[o][h, x, pair] = res[8 * main:].reshape(2, 4, over, WIDTH[o])

        @pl.when(s == 0)
        def _():
            pl.semaphore_wait(free, 21)

        for o in range(3):
            if over:
                to_sibling(s, o).start()
            each(s, o, lambda cp: cp.start())
        if over:
            @pl.when(s > 0)
            def _():
                merge(s - 1)
        return 0

    lax.fori_loop(0, 8, expert, 0)
    if over:
        merge(7)

    def returned(o):
        def one_block(s, _):
            each(s, o, lambda cp: cp.wait())
            if over:
                each_over(s, o, lambda cp: cp.wait())
                to_sibling(s, o).wait_send()
            return 0

        lax.fori_loop(0, 8, one_block, 0)

    token_row = lax.broadcasted_iota(jnp.int32, (2 * TOK, ROWS), 0).astype(F32) + 1.0

    FAR, DIRECT, SUM = range(3)

    def push(o, up, kind, turn):
        one, two, _ = WAYS[o]
        step, c = (1, 0) if up else (3, 1)
        a = (place[one] + turn) % 4
        group = (place[two] + (2 if kind == FAR else step)) % 4
        if kind == DIRECT:
            c = 1 - c
        slot = 2 if kind == FAR else step // 2
        at = kind if up else 3 + kind
        return remote(
            gs[o].at[group, a, c], acc2[o].at[slot, a, c],
            q2s.at[o, at, turn], q2r.at[o, at, turn], moved(place, two, step), core,
        )

    def combine(o, step):
        one, two, _ = WAYS[o]
        group = (place[two] + step) % 4
        for turn in (1, 3, 2, 0):
            a = (place[one] + turn) % 4
            index = tab2[o, group, pl.ds(a, 1), :ROWS]
            w = tab2[o, group, pl.ds(4 + a, 1), :ROWS]
            mix = jnp.where(index == token_row, w, 0.0).astype(BF16)
            rows = rs[o][:, group, a].reshape(8 * main, WIDTH[o])
            if over:
                rows = jnp.concatenate([rows, ro[o][:, group, a].reshape(4 * over, WIDTH[o])], axis=0)
            part = jnp.dot(mix, rows, preferred_element_type=F32)
            gs[o][group, a] = part.astype(BF16).reshape(2, TOK, WIDTH[o])
            if step == 2:
                push(o, True, FAR, turn).start()
                push(o, False, FAR, turn).start()
            elif step:
                push(o, step == 1, DIRECT, turn).start()

    returned(2)
    for step in (2, 1, 3, 0):
        combine(2, step)
    returned(0)
    returned(1)
    for step in (2, 1, 3, 0):
        combine(0, step)
        combine(1, step)

    for turn in (1, 3, 2, 0):
        for o in (2, 0, 1):
            one, two, _ = WAYS[o]
            a = (place[one] + turn) % 4
            for up in (True, False):
                step, c = (1, 0) if up else (3, 1)
                group = (place[two] + step) % 4
                push(o, up, FAR, turn).wait_recv()
                gs[o][group, a, c] = (gs[o][group, a, c].astype(F32) + acc2[o][2, a, c].astype(F32)).astype(BF16)
                push(o, up, SUM, turn).start()

    def reduce_first(o, step, cc):
        one, two, _ = WAYS[o]
        c = (core + cc) % 2
        return remote(
            gs[o].at[place[two], (place[one] + step) % 4, c], acc1[o].at[step, cc],
            q1s.at[o, step, cc], q1r.at[o, step, cc], moved(place, one, step), c,
        )

    for step in (1, 3, 2, 0):
        for o in (2, 0, 1):
            one, two, _ = WAYS[o]
            a = (place[one] + step) % 4
            for up in (True, False):
                push(o, up, FAR, step).wait_send()
                push(o, up, DIRECT, step).wait()
                push(o, up, SUM, step).wait()
            total = gs[o][place[two], a].astype(F32)
            for n in range(2):
                total += acc2[o][n, a].astype(F32)
            gs[o][place[two], a] = total.astype(BF16)
            for cc in range(2):
                if step or cc:
                    reduce_first(o, step, cc).start()
            if step == 0:
                acc1[o][0, 0] = gs[o][place[two], place[one], core]

    for o in (2, 0, 1):
        for step in range(4):
            for cc in range(2):
                if step or cc:
                    reduce_first(o, step, cc).wait()
        for cc in range(2):
            h = (core + cc) % 2
            where = pl.ds(pl.multiple_of(h * HALF + START[o], 128), WIDTH[o])
            total = acc1[o][0, cc].astype(F32)
            for step in (1, 2, 3):
                total += acc1[o][step, cc].astype(F32)
            out[:, where] = (resid[:, where].astype(F32) + total).astype(BF16)


def layer(main, over, number, resid, gain, ids, slots, wts, w_gate, w_up, w_down):
    vmem = pl.BlockSpec(memory_space=pltpu.VMEM)
    hbm = pl.BlockSpec(memory_space=pl.ANY)
    lanes = -(-(8 * main + 4 * over) // 128) * 128

    def per_way(*lead, rows):
        return [pltpu.VMEM((*lead, rows, w), BF16) for w in WIDTH]

    def pairs(*shapes):
        return [pltpu.SemaphoreType.DMA(shape) for shape in shapes for _ in range(2)]

    scratch = [
        *per_way(2, rows=TOK),
        *per_way(4, 4, 2, rows=TOK),
        *per_way(8, 4, 4, rows=main),
        *per_way(2, 4, 4, 4, rows=main),
        *per_way(3, 4, 2, rows=TOK),
        *per_way(4, 2, rows=TOK),
        pltpu.VMEM((3, 4, 8, lanes), F32),
        pltpu.VMEM((3, 4, 2, 8, lanes), F32),
        pltpu.VMEM((3, 4, 8, lanes), F32),
        pltpu.VMEM((3, 4, 8, lanes), F32),
        pltpu.VMEM((8 * (main + over), FF), BF16),
        pltpu.VMEM((D, FF), BF16),
        pltpu.VMEM((D, FF), BF16),
        pltpu.VMEM((FF, D), BF16),
        pltpu.SemaphoreType.DMA((3,)),
        *pairs((3, 4, 2), (3, 4, 2), (3, 4, 4), (3, 4), (3, 4, 2, 4), (8, 2), (8, 2, 2), (8, 4, 2), (3, 6, 4), (3, 4, 2)),
        pltpu.SemaphoreType.REGULAR,
    ]
    if over:
        scratch += [
            *per_way(4, 4, 4, rows=over),
            *per_way(2, 4, 4, 4, rows=over),
            *per_way(4, 4, 4, rows=over),
            *pairs((3, 4, 4), (3, 4, 4), (8,), (8, 2), (8, 4), (8, 3)),
        ]
    return pl.pallas_call(
        functools.partial(kernel, main, over),
        out_shape=(jax.ShapeDtypeStruct((TOK, D), BF16), jax.ShapeDtypeStruct((8, 128), F32)) if over
        else jax.ShapeDtypeStruct((TOK, D), BF16),
        in_specs=[vmem] * 5 + [hbm] * 3,
        out_specs=(vmem, vmem) if over else vmem,
        scratch_shapes=scratch,
        compiler_params=pltpu.CompilerParams(
            collective_id=number, has_side_effects=True, vmem_limit_bytes=62 * 2**20
        ),
        cost_estimate=pl.CostEstimate(flops=30 * 10**9, bytes_accessed=11 * 10**6, transcendentals=2 * 10**6),
    )(resid, gain, ids, slots, wts, w_gate, w_up, w_down)


def per_device(resid, norm_gain, w_gate, w_up, w_down, route_ids, route_slots, route_weights):
    args = (
        resid, norm_gain[None, :], route_ids.T, route_slots.T, route_weights.T, w_gate[0], w_up[0], w_down[0],
    )
    result, flag = layer(MAIN, OVER, 0, *args)
    return lax.cond(flag[0, 0] > 0.5, lambda result, *args: layer(2 * CAP, 0, 1, *args), lambda result, *args: result, result, *args)


def solution(mesh):
    rows = P(("dp", "expert"), None)
    expert = P(("dp", "expert"), None, None)
    return jax.shard_map(
        per_device, mesh=mesh, in_specs=(rows, P(), expert, expert, expert, rows, rows, rows), out_specs=rows, check_vma=False
    )
```

```python
import functools

import jax
import jax.numpy as jnp
from jax import lax
from jax.experimental import pallas as pl
from jax.experimental.pallas import tpu as pltpu
from jax.sharding import PartitionSpec as P

MESH = pl.DeviceIdType.MESH
F32 = jnp.float32
BF16 = jnp.bfloat16
epsilon = 1e-06

TOK = 128
D = 2048
FF = 768
FAN = 8
CAP = 20
MAIN = 24
OVER = 16
WAYS = ((2, 1, 0), (0, 2, 1), (1, 0, 2))
WIDTH = (384, 384, 256)
START = (0, 384, 768)
HALF = 1024


def my_place():
    dp = lax.axis_index("dp")
    ex = lax.axis_index("expert")
    return [(dp % 2) * 2 + ex // 2, (dp // 2) % 4, dp // 8], ex % 2


def device(place, core):
    x, y, z = place
    return (z * 8 + y * 2 + x // 2, (x % 2) * 2 + core)


def moved(place, axis, step):
    place = list(place)
    place[axis] = (place[axis] + step) % 4
    return place


def kernel(main, over, resid, gain, ids, slots, wts, wg_hbm, wu_hbm, wd_hbm, out, *scratch):
    if over:
        flag, *scratch = scratch
    it = iter(scratch)

    def take(n):
        return tuple(next(it) for _ in range(n))

    toks, gs, rs, xs, acc2, acc1 = (take(3) for _ in range(6))
    tab, tab1, tab2s, tab2, hidden, wg, wu, wd = take(8)
    sem_w, s1s, s1r, t1s, t1r, s2s, s2r, t2s, t2r, s3s, s3r, ras, rar, rbs, rbr, rcs, rcr, q2s, q2r, q1s, q1r, free = take(22)
    if over:
        ro, xo, ys = (take(3) for _ in range(3))
        s3os, s3or, fos, fors, oas, oar, obs, obr, ocs, ocr, yss, ysr = take(12)
    main_slots, over_slots = main // 2, over // 2
    ROWS = 8 * main + 4 * over
    LANES = tab.shape[-1]
    place, core = my_place()

    def remote(src, dst, ssem, rsem, where, c):
        return pltpu.make_async_remote_copy(
            src_ref=src, dst_ref=dst, send_sem=ssem, recv_sem=rsem,
            device_id=device(where, c), device_id_type=MESH,
        )

    loads = [pltpu.make_async_copy(h, v, sem_w.at[i]) for i, (h, v) in enumerate(((wg_hbm, wg), (wu_hbm, wu), (wd_hbm, wd)))]
    for cp in loads:
        cp.start()

    barrier = pltpu.get_barrier_semaphore()
    for axis in range(3):
        for step in (1, 2, 3):
            for c in range(2):
                pl.semaphore_signal(barrier, inc=1, device_id=device(moved(place, axis, step), c), device_id_type=MESH)
    pl.semaphore_signal(barrier, inc=1, device_id=device(place, 1 - core), device_id_type=MESH)

    floats = resid[...].astype(F32)
    mean_square = jnp.mean(floats * floats, axis=1, keepdims=True)
    normed = (floats * lax.rsqrt(mean_square + epsilon) * gain[...]).astype(BF16)
    for o in range(3):
        for h in range(2):
            lo = h * HALF + START[o]
            toks[o][h] = normed[:, lo:lo + WIDTH[o]]

    pl.semaphore_wait(barrier, 19)

    def first(o, step, cc):
        one, two, _ = WAYS[o]
        h = (core + cc) % 2
        return remote(
            toks[o].at[h], gs[o].at[place[two], place[one], core],
            s1s.at[o, step, cc], s1r.at[o, step, cc], moved(place, one, step), h,
        )

    for step in (1, 3, 2, 0):
        for o in range(3):
            for cc in range(2):
                if step or cc:
                    first(o, step, cc).start()
    for o in range(3):
        one, two, _ = WAYS[o]
        gs[o][place[two], place[one], core] = toks[o][core]

    e = ids[...]
    coords = ((e >> 1) & 3, (e >> 3) & 3, e >> 5)
    sl = slots[...]
    lane = lax.broadcasted_iota(jnp.int32, (TOK, LANES), 1).astype(F32)
    level = lax.broadcasted_iota(jnp.int32, (32, TOK), 0)
    number = (lax.broadcasted_iota(jnp.int32, (TOK, 1), 0) + 1 + core * TOK).astype(F32)
    weight = wts[...].T
    for o in range(3):
        one, two, three = WAYS[o]
        spot = ((coords[three] * 2 + (e & 1)) * 2 + core) * main_slots + sl
        if over:
            shared = 8 * main + (coords[three] * 2 + core) * over_slots + sl - main_slots
            spot = jnp.where(sl < main_slots, spot, shared)
        spot = jnp.where(sl >= 0, spot, -1).astype(F32).T
        line = coords[one] * 8 + coords[two]
        total = jnp.zeros((32, LANES), F32)
        for k in range(FAN):
            hit = lane == spot[:, k:k + 1]
            here = level == line[k:k + 1]
            there = level == line[k:k + 1] + 4
            for mask, value in ((here, number), (there, weight[:, k:k + 1])):
                total += jnp.dot(
                    mask.astype(F32).astype(BF16), jnp.where(hit, value, 0.0).astype(BF16), preferred_element_type=F32
                )
        tab[o] = total.reshape(4, 8, LANES)

    if over:
        number_e = lax.broadcasted_iota(jnp.int32, (2, 64, TOK), 1) * 2 + lax.broadcasted_iota(jnp.int32, (2, 64, TOK), 0)
        seen = jnp.zeros((2, 64, TOK), F32)
        for k in range(FAN):
            past = (sl[k:k + 1] >= main_slots)[None]
            seen = jnp.where((number_e == e[k:k + 1][None]) & past, 1.0, seen)
        seen = jnp.max(seen, axis=2, keepdims=True)
        flag[...] = jnp.broadcast_to(jnp.max(seen[0] * seen[1], axis=0, keepdims=True), flag.shape)

    def first_table(o, step, cc):
        one, _, _ = WAYS[o]
        return remote(
            tab.at[o, (place[one] + step) % 4], tab1.at[o, place[one], core],
            t1s.at[o, step, cc], t1r.at[o, step, cc], moved(place, one, step), (core + cc) % 2,
        )

    for o in range(3):
        one, _, _ = WAYS[o]
        for step in (1, 3, 2, 0):
            for cc in range(2):
                if step or cc:
                    first_table(o, step, cc).start()
        tab1[o, place[one], core] = tab[o, place[one]]

    def second(o, step, back):
        one, two, _ = WAYS[o]
        piece = gs[o].at[place[two], (place[one] + 4 - back) % 4]
        return remote(piece, piece, s2s.at[o, step, back], s2r.at[o, step, back], moved(place, two, step), core)

    def forward(o, up, back):
        one, two, _ = WAYS[o]
        piece = gs[o].at[(place[two] + (3 if up else 1)) % 4, (place[one] + 4 - back) % 4, 0 if up else 1]
        at = 0 if up else 2
        return remote(piece, piece, s2s.at[o, at, back], s2r.at[o, at, back], moved(place, two, 1 if up else 3), core)

    def second_wait(o, step, back):
        one, two, _ = WAYS[o]
        came = gs[o].at[(place[two] + 4 - step) % 4, (place[one] + 4 - back) % 4]
        remote(came, came, s2s.at[o, step, back], s2r.at[o, step, back], place, core).wait_recv()

    def forward_wait(o, up, back):
        one, two, _ = WAYS[o]
        at = 0 if up else 2
        came = gs[o].at[(place[two] + 2) % 4, (place[one] + 4 - back) % 4, 0 if up else 1]
        remote(came, came, s2s.at[o, at, back], s2r.at[o, at, back], place, core).wait_recv()

    def second_table(o, step):
        two = WAYS[o][1]
        return remote(
            tab2s.at[o, (place[two] + step) % 4], tab2.at[o, place[two]],
            t2s.at[o, step], t2r.at[o, step], moved(place, two, step), core,
        )

    def first_wait(o, step, cc):
        one, two, _ = WAYS[o]
        came = gs[o].at[place[two], (place[one] + 4 - step) % 4, (core + cc) % 2]
        remote(came, came, s1s.at[o, step, cc], s1r.at[o, step, cc], place, core).wait_recv()

    def first_table_wait(o, step, cc):
        one, _, _ = WAYS[o]
        came = tab1.at[o, (place[one] + 4 - step) % 4, (core + cc) % 2]
        remote(came, came, t1s.at[o, step, cc], t1r.at[o, step, cc], place, core).wait_recv()

    for back in (0, 1, 3, 2):
        for o in range(3):
            for cc in range(2):
                if back or cc:
                    first_wait(o, back, cc)
            for step in (1, 3):
                second(o, step, back).start()
    for o in range(3):
        for step in (0, 1, 3, 2):
            for cc in range(2):
                if step or cc:
                    first_table_wait(o, step, cc)
        for line in range(4):
            for a in range(4):
                tab2s[o, line, a:a + 1] = tab1[o, a, 0, line:line + 1] + tab1[o, a, 1, line:line + 1]
                tab2s[o, line, 4 + a:5 + a] = tab1[o, a, 0, 4 + line:5 + line] + tab1[o, a, 1, 4 + line:5 + line]
        for step in (1, 3, 2):
            second_table(o, step).start()
        two = WAYS[o][1]
        tab2[o, place[two]] = tab2s[o, place[two]]

    def landing(o, frm, group, to):
        if o == 0:
            return lambda h: to[0].at[h, frm, group]
        if o == 1:
            return lambda h: to[1].at[h, :, frm, group]
        return lambda h: to[2].at[h, group, :, frm]

    def third(o, step, cc, n, group):
        three = WAYS[o][2]
        to = (place[three] + step) % 4
        c = (core + cc) % 2
        src = rs[o].at[to * 2 + c, group]
        dst = landing(o, place[three], group, xs)(core)
        if step == 0 and cc == 0:
            return pltpu.make_async_copy(src, dst, s3r.at[o, 0, 0, n])
        return remote(src, dst, s3s.at[o, step, cc, n], s3r.at[o, step, cc, n], moved(place, three, step), c)

    def third_over(o, step, n, group):
        three = WAYS[o][2]
        src = ro[o].at[(place[three] + step) % 4, group]
        dst = landing(o, place[three], group, xo)(core)
        if step == 0:
            return pltpu.make_async_copy(src, dst, s3or.at[o, 0, n])
        return remote(src, dst, s3os.at[o, step, n], s3or.at[o, step, n], moved(place, three, step), core)

    def across(o, step, n, group, h):
        came = landing(o, (place[WAYS[o][2]] + 4 - step) % 4, group, xo)(h)
        return remote(came, came, fos.at[o, step, n], fors.at[o, step, n], place, 1 - core)

    def group_of(o, n):
        two = WAYS[o][1]
        gap = n ^ (n >> 1)
        return gap, (place[two] + 4 - gap) % 4

    token_lane = lax.broadcasted_iota(jnp.int32, (ROWS, 2 * TOK), 1).astype(F32) + 1.0

    def pack(o, n):
        three = WAYS[o][2]
        gap, group = group_of(o, n)
        column = tab2[o, group].T
        for a in range(4):
            pick = jnp.where(column[:ROWS, a:a + 1] == token_lane, 1.0, 0.0).astype(BF16)
            rows = jnp.dot(pick, gs[o][group, a].reshape(2 * TOK, WIDTH[o]), preferred_element_type=F32)
            rows = rows.astype(BF16)
            rs[o][:, group, a] = rows[:8 * main].reshape(8, main, WIDTH[o])
            if over:
                ro[o][:, group, a] = rows[8 * main:].reshape(4, over, WIDTH[o])
        for step in (1, 3, 2, 0):
            if over:
                third_over(o, step, n, group).start()
            for cc in range(2):
                third(o, step, cc, n, group).start()

    for o in range(3):
        pack(o, 0)
    for back in (0, 1, 3, 2):
        for o in range(3):
            for step in (1, 3):
                second_wait(o, step, back)
                forward(o, step == 1, back).start()

    def others(n, _):
        for o in range(3):
            gap, group = group_of(o, n)

            @pl.when(n == 3)
            def _():
                for back in range(4):
                    forward_wait(o, True, back)
                    forward_wait(o, False, back)

            came = tab2.at[o, group]
            remote(came, came, t2s.at[o, gap], t2r.at[o, gap], place, core).wait_recv()
            pack(o, n)
        return 0

    lax.fori_loop(1, 4, others, 0)

    for o in range(3):
        for step in range(4):
            for cc in range(2):
                if step or cc:
                    first(o, step, cc).wait_send()
                    first_table(o, step, cc).wait_send()
            if step:
                second_table(o, step).wait_send()
        for back in range(4):
            for step in (1, 3):
                second(o, step, back).wait_send()
                forward(o, step == 1, back).wait_send()

    for cp in loads:
        cp.wait()

    def shared_arrive(n, _):
        for o in range(3):
            gap, group = group_of(o, n)
            for step in range(4):
                if step == 0:
                    third_over(o, 0, n, group).wait()
                else:
                    came = landing(o, (place[WAYS[o][2]] + 4 - step) % 4, group, xo)(core)
                    remote(came, came, s3os.at[o, step, n], s3or.at[o, step, n], place, core).wait_recv()
                    third_over(o, step, n, group).wait_send()
                across(o, step, n, group, core).start()
        return 0

    def arrive(n, _):
        for o in range(3):
            three = WAYS[o][2]
            gap, group = group_of(o, n)
            for step in range(4):
                for cc in range(2):
                    came = landing(o, (place[three] + 4 - step) % 4, group, xs)((core + cc) % 2)
                    if step == 0 and cc == 0:
                        third(o, 0, 0, n, group).wait()
                    else:
                        remote(came, came, s3s.at[o, step, cc, n], s3r.at[o, step, cc, n], place, core).wait_recv()
                        third(o, step, cc, n, group).wait_send()
                if over:
                    across(o, step, n, group, core).wait_send()
                    across(o, step, n, group, 1 - core).wait_recv()
        return 0

    if over:
        lax.fori_loop(0, 4, shared_arrive, 0)
    lax.fori_loop(0, 4, arrive, 0)

    for o in range(3):
        for step in range(4):
            for cc in range(2):
                if step or cc:
                    pl.semaphore_signal(
                        free, inc=1, device_id=device(moved(place, WAYS[o][2], step), (core + cc) % 2), device_id_type=MESH
                    )

    mx, my, mz = place

    def send_a(s, x, q, cc, local):
        h = (core + cc) % 2
        src = xs[0].at[h, x, pl.ds(2 * q, 2)]
        dst = rs[0].at[mx * 2 + core, pl.ds(2 * q, 2)]
        if local:
            return pltpu.make_async_copy(src, dst, rar.at[s, cc])
        return remote(src, dst, ras.at[s, cc], rar.at[s, cc], (x, my, mz), h)

    def send_b(s, x, q, i, cc, local):
        h = (core + cc) % 2
        y = 2 * q + (my + i) % 2
        src = xs[1].at[h, x, y]
        dst = rs[1].at[my * 2 + core, :, x]
        if local:
            return pltpu.make_async_copy(src, dst, rbr.at[s, i, cc])
        return remote(src, dst, rbs.at[s, i, cc], rbr.at[s, i, cc], (mx, y, mz), h)

    def send_c(s, x, q, step, cc):
        h = (core + cc) % 2
        z = (mz + step) % 4
        src = xs[2].at[h, x, pl.ds(2 * q, 2), z]
        dst = rs[2].at[mz * 2 + core, x, pl.ds(2 * q, 2)]
        if step == 0 and cc == 0:
            return pltpu.make_async_copy(src, dst, rcr.at[s, 0, 0])
        return remote(src, dst, rcs.at[s, step, cc], rcr.at[s, step, cc], (mx, my, z), h)

    def over_a(s, x, q, local):
        src, dst = xo[0].at[core, x, pl.ds(2 * q, 2)], ro[0].at[mx, pl.ds(2 * q, 2)]
        if local:
            return pltpu.make_async_copy(src, dst, oar.at[s])
        return remote(src, dst, oas.at[s], oar.at[s], (x, my, mz), core)

    def over_b(s, x, q, i, local):
        y = 2 * q + (my + i) % 2
        src, dst = xo[1].at[core, x, y], ro[1].at[my, :, x]
        if local:
            return pltpu.make_async_copy(src, dst, obr.at[s, i])
        return remote(src, dst, obs.at[s, i], obr.at[s, i], (mx, y, mz), core)

    def over_c(s, x, q, step):
        z = (mz + step) % 4
        src, dst = xo[2].at[core, x, pl.ds(2 * q, 2), z], ro[2].at[mz, x, pl.ds(2 * q, 2)]
        if step == 0:
            return pltpu.make_async_copy(src, dst, ocr.at[s, 0])
        return remote(src, dst, ocs.at[s, step], ocr.at[s, step], (mx, my, z), core)

    def each_over(s, o, act):
        x, q = block_of(s)
        if o == 0:
            @pl.when(s % 4 < 3)
            def _():
                act(over_a(s, x, q, False))

            @pl.when(s % 4 == 3)
            def _():
                act(over_a(s, x, q, True))
        elif o == 1:
            act(over_b(s, x, q, 1, False))

            @pl.when(s < 4)
            def _():
                act(over_b(s, x, q, 0, False))

            @pl.when(s >= 4)
            def _():
                act(over_b(s, x, q, 0, True))
        else:
            for step in (1, 3, 2, 0):
                act(over_c(s, x, q, step))

    def to_sibling(s, o):
        x, q = block_of(s)
        return remote(
            xo[o].at[1 - core, x, pl.ds(2 * q, 2)], ys[o].at[x, pl.ds(2 * q, 2)],
            yss.at[s, o], ysr.at[s, o], place, 1 - core,
        )

    def merge(s):
        x, q = block_of(s)
        pair = pl.ds(2 * q, 2)
        for o in range(3):
            to_sibling(s, o).wait_recv()
            mine = xo[o][core, x, pair].reshape(8 * over, WIDTH[o]).astype(F32)
            theirs = ys[o][x, pair].reshape(8 * over, WIDTH[o]).astype(F32)
            kept = jnp.where(hot > 0.0, mine, theirs).astype(BF16)
            xo[o][core, x, pair] = kept.reshape(2, 4, over, WIDTH[o])
            each_over(s, o, lambda cp: cp.start())

    if over:
        me = ((mz * 4 + my) * 4 + mx) * 2 + core
        filled = jnp.where((ids[...] == me) & (slots[...] >= main_slots), 1.0, 0.0)
        hot = jnp.max(jnp.max(filled, axis=1, keepdims=True), axis=0, keepdims=True)

    def block_of(s):
        turn = (s + 1) % 4
        return (mx + (turn ^ (turn >> 1))) % 4, (my // 2 + 1 - s // 4) % 2

    def each(s, o, act):
        x, q = block_of(s)
        for cc in range(2):
            if o == 0 and cc:
                act(send_a(s, x, q, cc, False))
            elif o == 0:
                @pl.when(s % 4 < 3)
                def _():
                    act(send_a(s, x, q, 0, False))

                @pl.when(s % 4 == 3)
                def _():
                    act(send_a(s, x, q, 0, True))
            elif o == 1:
                for i in range(2):
                    if cc or i:
                        act(send_b(s, x, q, i, cc, False))
                    else:
                        @pl.when(s < 4)
                        def _():
                            act(send_b(s, x, q, 0, 0, False))

                        @pl.when(s >= 4)
                        def _():
                            act(send_b(s, x, q, 0, 0, True))
            else:
                for step in (1, 3, 2, 0):
                    act(send_c(s, x, q, step, cc))

    def expert(s, _):
        x, q = block_of(s)
        pair = pl.ds(2 * q, 2)
        halves = [(h, o) for h in range(2) for o in range(3)]
        rows = jnp.concatenate([xs[o][h, x, pair].reshape(8 * main, WIDTH[o]) for h, o in halves], axis=1)
        if over:
            shared = jnp.concatenate([xo[o][h, x, pair].reshape(8 * over, WIDTH[o]) for h, o in halves], axis=1)
            rows = jnp.concatenate([rows, shared], axis=0)
        for f in range(0, FF, 256):
            gate = jnp.dot(rows, wg[:, f:f + 256], preferred_element_type=F32)
            up = jnp.dot(rows, wu[:, f:f + 256], preferred_element_type=F32)
            hidden[:, f:f + 256] = (gate / (1.0 + jnp.exp(-gate)) * up).astype(BF16)
        for h in range(2):
            for o in range(3):
                lo = h * HALF + START[o]
                res = jnp.dot(hidden[...], wd[:, lo:lo + WIDTH[o]], preferred_element_type=F32)
                res = res.astype(BF16)
                xs[o][h, x, pair] = res[:8 * main].reshape(2, 4, main, WIDTH[o])
                if over:
                    xo[o][h, x, pair] = res[8 * main:].reshape(2, 4, over, WIDTH[o])

        @pl.when(s == 0)
        def _():
            pl.semaphore_wait(free, 21)

        for o in range(3):
            if over:
                to_sibling(s, o).start()
            each(s, o, lambda cp: cp.start())
        if over:
            @pl.when(s > 0)
            def _():
                merge(s - 1)
        return 0

    lax.fori_loop(0, 8, expert, 0)
    if over:
        merge(7)

    def returned(o, begin=0, end=8):
        def one_block(s, _):
            each(s, o, lambda cp: cp.wait())
            if over:
                each_over(s, o, lambda cp: cp.wait())
                to_sibling(s, o).wait_send()
            return 0

        lax.fori_loop(begin, end, one_block, 0)

    token_row = lax.broadcasted_iota(jnp.int32, (2 * TOK, ROWS), 0).astype(F32) + 1.0

    FAR, DIRECT, SUM = range(3)

    def push(o, up, kind, turn):
        one, two, _ = WAYS[o]
        step, c = (1, 0) if up else (3, 1)
        a = (place[one] + turn) % 4
        group = (place[two] + (2 if kind == FAR else step)) % 4
        if kind == DIRECT:
            c = 1 - c
        slot = 2 if kind == FAR else step // 2
        at = kind if up else 3 + kind
        return remote(
            gs[o].at[group, a, c], acc2[o].at[slot, a, c],
            q2s.at[o, at, turn], q2r.at[o, at, turn], moved(place, two, step), core,
        )

    def combine(o, step):
        one, two, _ = WAYS[o]
        group = (place[two] + step) % 4
        for turn in (1, 3, 2, 0):
            a = (place[one] + turn) % 4
            index = tab2[o, group, pl.ds(a, 1), :ROWS]
            w = tab2[o, group, pl.ds(4 + a, 1), :ROWS]
            mix = jnp.where(index == token_row, w, 0.0).astype(BF16)
            rows = rs[o][:, group, a].reshape(8 * main, WIDTH[o])
            if over:
                rows = jnp.concatenate([rows, ro[o][:, group, a].reshape(4 * over, WIDTH[o])], axis=0)
            part = jnp.dot(mix, rows, preferred_element_type=F32)
            gs[o][group, a] = part.astype(BF16).reshape(2, TOK, WIDTH[o])
            if step == 2:
                push(o, True, FAR, turn).start()
                push(o, False, FAR, turn).start()
            elif step:
                push(o, step == 1, DIRECT, turn).start()

    returned(0, 0, 4)
    combine(0, 2)
    returned(2)
    for step in (2, 1, 3, 0):
        combine(2, step)
    returned(0, 4, 8)
    returned(1)
    combine(1, 2)
    for step in (1, 3, 0):
        combine(0, step)
        combine(1, step)

    for turn in (1, 3, 2, 0):
        for o in (2, 0, 1):
            one, two, _ = WAYS[o]
            a = (place[one] + turn) % 4
            for up in (True, False):
                step, c = (1, 0) if up else (3, 1)
                group = (place[two] + step) % 4
                push(o, up, FAR, turn).wait_recv()
                gs[o][group, a, c] = (gs[o][group, a, c].astype(F32) + acc2[o][2, a, c].astype(F32)).astype(BF16)
                push(o, up, SUM, turn).start()

    def reduce_first(o, step, cc):
        one, two, _ = WAYS[o]
        c = (core + cc) % 2
        return remote(
            gs[o].at[place[two], (place[one] + step) % 4, c], acc1[o].at[step, cc],
            q1s.at[o, step, cc], q1r.at[o, step, cc], moved(place, one, step), c,
        )

    for step in (1, 3, 2, 0):
        for o in (2, 0, 1):
            one, two, _ = WAYS[o]
            a = (place[one] + step) % 4
            for up in (True, False):
                push(o, up, FAR, step).wait_send()
                push(o, up, DIRECT, step).wait()
                push(o, up, SUM, step).wait()
            total = gs[o][place[two], a].astype(F32)
            for n in range(2):
                total += acc2[o][n, a].astype(F32)
            gs[o][place[two], a] = total.astype(BF16)
            for cc in range(2):
                if step or cc:
                    reduce_first(o, step, cc).start()
            if step == 0:
                acc1[o][0, 0] = gs[o][place[two], place[one], core]

    for o in (2, 0, 1):
        for step in range(4):
            for cc in range(2):
                if step or cc:
                    reduce_first(o, step, cc).wait()
        for cc in range(2):
            h = (core + cc) % 2
            where = pl.ds(pl.multiple_of(h * HALF + START[o], 128), WIDTH[o])
            total = acc1[o][0, cc].astype(F32)
            for step in (1, 2, 3):
                total += acc1[o][step, cc].astype(F32)
            out[:, where] = (resid[:, where].astype(F32) + total).astype(BF16)


def layer(main, over, number, resid, gain, ids, slots, wts, w_gate, w_up, w_down):
    vmem = pl.BlockSpec(memory_space=pltpu.VMEM)
    hbm = pl.BlockSpec(memory_space=pl.ANY)
    lanes = -(-(8 * main + 4 * over) // 128) * 128

    def per_way(*lead, rows):
        return [pltpu.VMEM((*lead, rows, w), BF16) for w in WIDTH]

    def pairs(*shapes):
        return [pltpu.SemaphoreType.DMA(shape) for shape in shapes for _ in range(2)]

    scratch = [
        *per_way(2, rows=TOK),
        *per_way(4, 4, 2, rows=TOK),
        *per_way(8, 4, 4, rows=main),
        *per_way(2, 4, 4, 4, rows=main),
        *per_way(3, 4, 2, rows=TOK),
        *per_way(4, 2, rows=TOK),
        pltpu.VMEM((3, 4, 8, lanes), F32),
        pltpu.VMEM((3, 4, 2, 8, lanes), F32),
        pltpu.VMEM((3, 4, 8, lanes), F32),
        pltpu.VMEM((3, 4, 8, lanes), F32),
        pltpu.VMEM((8 * (main + over), FF), BF16),
        pltpu.VMEM((D, FF), BF16),
        pltpu.VMEM((D, FF), BF16),
        pltpu.VMEM((FF, D), BF16),
        pltpu.SemaphoreType.DMA((3,)),
        *pairs((3, 4, 2), (3, 4, 2), (3, 4, 4), (3, 4), (3, 4, 2, 4), (8, 2), (8, 2, 2), (8, 4, 2), (3, 6, 4), (3, 4, 2)),
        pltpu.SemaphoreType.REGULAR,
    ]
    if over:
        scratch += [
            *per_way(4, 4, 4, rows=over),
            *per_way(2, 4, 4, 4, rows=over),
            *per_way(4, 4, 4, rows=over),
            *pairs((3, 4, 4), (3, 4, 4), (8,), (8, 2), (8, 4), (8, 3)),
        ]
    return pl.pallas_call(
        functools.partial(kernel, main, over),
        out_shape=(jax.ShapeDtypeStruct((TOK, D), BF16), jax.ShapeDtypeStruct((8, 128), F32)) if over
        else jax.ShapeDtypeStruct((TOK, D), BF16),
        in_specs=[vmem] * 5 + [hbm] * 3,
        out_specs=(vmem, vmem) if over else vmem,
        scratch_shapes=scratch,
        compiler_params=pltpu.CompilerParams(
            collective_id=number, has_side_effects=True, vmem_limit_bytes=62 * 2**20
        ),
        cost_estimate=pl.CostEstimate(flops=30 * 10**9, bytes_accessed=11 * 10**6, transcendentals=2 * 10**6),
    )(resid, gain, ids, slots, wts, w_gate, w_up, w_down)


def per_device(resid, norm_gain, w_gate, w_up, w_down, route_ids, route_slots, route_weights):
    args = (
        resid, norm_gain[None, :], route_ids.T, route_slots.T, route_weights.T, w_gate[0], w_up[0], w_down[0],
    )
    result, flag = layer(MAIN, OVER, 0, *args)
    return lax.cond(flag[0, 0] > 0.5, lambda result, *args: layer(2 * CAP, 0, 1, *args), lambda result, *args: result, result, *args)


def solution(mesh):
    rows = P(("dp", "expert"), None)
    expert = P(("dp", "expert"), None, None)
    return jax.shard_map(
        per_device, mesh=mesh, in_specs=(rows, P(), expert, expert, expert, rows, rows, rows), out_specs=rows, check_vma=False
    )
```

```python
import functools

import jax
import jax.numpy as jnp
from jax import lax
from jax.experimental import pallas as pl
from jax.experimental.pallas import tpu as pltpu
from jax.sharding import PartitionSpec as P

MESH = pl.DeviceIdType.MESH
F32 = jnp.float32
BF16 = jnp.bfloat16
epsilon = 1e-06

TOK = 128
D = 2048
FF = 768
FAN = 8
CAP = 20
MAIN = 24
OVER = 16
WAYS = ((2, 1, 0), (0, 2, 1), (1, 0, 2))
WIDTH = (384, 384, 256)
START = (0, 384, 768)
HALF = 1024


def my_place():
    dp = lax.axis_index("dp")
    ex = lax.axis_index("expert")
    return [(dp % 2) * 2 + ex // 2, (dp // 2) % 4, dp // 8], ex % 2


def device(place, core):
    x, y, z = place
    return (z * 8 + y * 2 + x // 2, (x % 2) * 2 + core)


def moved(place, axis, step):
    place = list(place)
    place[axis] = (place[axis] + step) % 4
    return place


def kernel(main, over, resid, gain, ids, slots, wts, wg_hbm, wu_hbm, wd_hbm, out, *scratch):
    if over:
        flag, *scratch = scratch
    it = iter(scratch)

    def take(n):
        return tuple(next(it) for _ in range(n))

    toks, gs, rs, xs, acc2, acc1 = (take(3) for _ in range(6))
    tab, tab1, tab2s, tab2, hidden, wg, wu, wd = take(8)
    sem_w, s1s, s1r, t1s, t1r, s2s, s2r, t2s, t2r, s3s, s3r, ras, rar, rbs, rbr, rcs, rcr, q2s, q2r, q1s, q1r, free = take(22)
    if over:
        ro, xo, ys = (take(3) for _ in range(3))
        s3os, s3or, fos, fors, oas, oar, obs, obr, ocs, ocr, yss, ysr = take(12)
    main_slots, over_slots = main // 2, over // 2
    ROWS = 8 * main + 4 * over
    LANES = tab.shape[-1]
    place, core = my_place()

    def remote(src, dst, ssem, rsem, where, c):
        return pltpu.make_async_remote_copy(
            src_ref=src, dst_ref=dst, send_sem=ssem, recv_sem=rsem,
            device_id=device(where, c), device_id_type=MESH,
        )

    loads = [pltpu.make_async_copy(h, v, sem_w.at[i]) for i, (h, v) in enumerate(((wg_hbm, wg), (wu_hbm, wu), (wd_hbm, wd)))]
    for cp in loads:
        cp.start()

    barrier = pltpu.get_barrier_semaphore()
    for axis in range(3):
        for step in (1, 2, 3):
            for c in range(2):
                pl.semaphore_signal(barrier, inc=1, device_id=device(moved(place, axis, step), c), device_id_type=MESH)
    pl.semaphore_signal(barrier, inc=1, device_id=device(place, 1 - core), device_id_type=MESH)

    floats = resid[...].astype(F32)
    mean_square = jnp.mean(floats * floats, axis=1, keepdims=True)
    normed = (floats * lax.rsqrt(mean_square + epsilon) * gain[...]).astype(BF16)
    for o in range(3):
        for h in range(2):
            lo = h * HALF + START[o]
            toks[o][h] = normed[:, lo:lo + WIDTH[o]]

    pl.semaphore_wait(barrier, 19)

    def first(o, step, cc):
        one, two, _ = WAYS[o]
        h = (core + cc) % 2
        return remote(
            toks[o].at[h], gs[o].at[place[two], place[one], core],
            s1s.at[o, step, cc], s1r.at[o, step, cc], moved(place, one, step), h,
        )

    for step in (1, 3, 2, 0):
        for o in range(3):
            for cc in range(2):
                if step or cc:
                    first(o, step, cc).start()
    for o in range(3):
        one, two, _ = WAYS[o]
        gs[o][place[two], place[one], core] = toks[o][core]

    e = ids[...]
    coords = ((e >> 1) & 3, (e >> 3) & 3, e >> 5)
    sl = slots[...]
    lane = lax.broadcasted_iota(jnp.int32, (TOK, LANES), 1).astype(F32)
    level = lax.broadcasted_iota(jnp.int32, (32, TOK), 0)
    number = (lax.broadcasted_iota(jnp.int32, (TOK, 1), 0) + 1 + core * TOK).astype(F32)
    weight = wts[...].T
    for o in range(3):
        one, two, three = WAYS[o]
        spot = ((coords[three] * 2 + (e & 1)) * 2 + core) * main_slots + sl
        if over:
            shared = 8 * main + (coords[three] * 2 + core) * over_slots + sl - main_slots
            spot = jnp.where(sl < main_slots, spot, shared)
        spot = jnp.where(sl >= 0, spot, -1).astype(F32).T
        line = coords[one] * 8 + coords[two]
        total = jnp.zeros((32, LANES), F32)
        for k in range(FAN):
            hit = lane == spot[:, k:k + 1]
            here = level == line[k:k + 1]
            there = level == line[k:k + 1] + 4
            for mask, value in ((here, number), (there, weight[:, k:k + 1])):
                total += jnp.dot(
                    mask.astype(F32).astype(BF16), jnp.where(hit, value, 0.0).astype(BF16), preferred_element_type=F32
                )
        tab[o] = total.reshape(4, 8, LANES)

    if over:
        number_e = lax.broadcasted_iota(jnp.int32, (2, 64, TOK), 1) * 2 + lax.broadcasted_iota(jnp.int32, (2, 64, TOK), 0)
        seen = jnp.zeros((2, 64, TOK), F32)
        for k in range(FAN):
            past = (sl[k:k + 1] >= main_slots)[None]
            seen = jnp.where((number_e == e[k:k + 1][None]) & past, 1.0, seen)
        seen = jnp.max(seen, axis=2, keepdims=True)
        flag[...] = jnp.broadcast_to(jnp.max(seen[0] * seen[1], axis=0, keepdims=True), flag.shape)

    def first_table(o, step, cc):
        one, _, _ = WAYS[o]
        return remote(
            tab.at[o, (place[one] + step) % 4], tab1.at[o, place[one], core],
            t1s.at[o, step, cc], t1r.at[o, step, cc], moved(place, one, step), (core + cc) % 2,
        )

    for o in range(3):
        one, _, _ = WAYS[o]
        for step in (1, 3, 2, 0):
            for cc in range(2):
                if step or cc:
                    first_table(o, step, cc).start()
        tab1[o, place[one], core] = tab[o, place[one]]

    def second(o, step, back):
        one, two, _ = WAYS[o]
        piece = gs[o].at[place[two], (place[one] + 4 - back) % 4]
        return remote(piece, piece, s2s.at[o, step, back], s2r.at[o, step, back], moved(place, two, step), core)

    def forward(o, up, back):
        one, two, _ = WAYS[o]
        piece = gs[o].at[(place[two] + (3 if up else 1)) % 4, (place[one] + 4 - back) % 4, 0 if up else 1]
        at = 0 if up else 2
        return remote(piece, piece, s2s.at[o, at, back], s2r.at[o, at, back], moved(place, two, 1 if up else 3), core)

    def second_wait(o, step, back):
        one, two, _ = WAYS[o]
        came = gs[o].at[(place[two] + 4 - step) % 4, (place[one] + 4 - back) % 4]
        remote(came, came, s2s.at[o, step, back], s2r.at[o, step, back], place, core).wait_recv()

    def forward_wait(o, up, back):
        one, two, _ = WAYS[o]
        at = 0 if up else 2
        came = gs[o].at[(place[two] + 2) % 4, (place[one] + 4 - back) % 4, 0 if up else 1]
        remote(came, came, s2s.at[o, at, back], s2r.at[o, at, back], place, core).wait_recv()

    def second_table(o, step):
        two = WAYS[o][1]
        return remote(
            tab2s.at[o, (place[two] + step) % 4], tab2.at[o, place[two]],
            t2s.at[o, step], t2r.at[o, step], moved(place, two, step), core,
        )

    def first_wait(o, step, cc):
        one, two, _ = WAYS[o]
        came = gs[o].at[place[two], (place[one] + 4 - step) % 4, (core + cc) % 2]
        remote(came, came, s1s.at[o, step, cc], s1r.at[o, step, cc], place, core).wait_recv()

    def first_table_wait(o, step, cc):
        one, _, _ = WAYS[o]
        came = tab1.at[o, (place[one] + 4 - step) % 4, (core + cc) % 2]
        remote(came, came, t1s.at[o, step, cc], t1r.at[o, step, cc], place, core).wait_recv()

    for back in (0, 1, 3, 2):
        for o in range(3):
            for cc in range(2):
                if back or cc:
                    first_wait(o, back, cc)
            for step in (1, 3):
                second(o, step, back).start()
    for o in range(3):
        for step in (0, 1, 3, 2):
            for cc in range(2):
                if step or cc:
                    first_table_wait(o, step, cc)
        for line in range(4):
            for a in range(4):
                tab2s[o, line, a:a + 1] = tab1[o, a, 0, line:line + 1] + tab1[o, a, 1, line:line + 1]
                tab2s[o, line, 4 + a:5 + a] = tab1[o, a, 0, 4 + line:5 + line] + tab1[o, a, 1, 4 + line:5 + line]
        for step in (1, 3, 2):
            second_table(o, step).start()
        two = WAYS[o][1]
        tab2[o, place[two]] = tab2s[o, place[two]]

    def landing(o, frm, group, to):
        if o == 0:
            return lambda h: to[0].at[h, frm, group]
        if o == 1:
            return lambda h: to[1].at[h, :, frm, group]
        return lambda h: to[2].at[h, group, :, frm]

    def third(o, step, cc, n, group):
        three = WAYS[o][2]
        to = (place[three] + step) % 4
        c = (core + cc) % 2
        src = rs[o].at[to * 2 + c, group]
        dst = landing(o, place[three], group, xs)(core)
        if step == 0 and cc == 0:
            return pltpu.make_async_copy(src, dst, s3r.at[o, 0, 0, n])
        return remote(src, dst, s3s.at[o, step, cc, n], s3r.at[o, step, cc, n], moved(place, three, step), c)

    def third_over(o, step, n, group):
        three = WAYS[o][2]
        src = ro[o].at[(place[three] + step) % 4, group]
        dst = landing(o, place[three], group, xo)(core)
        if step == 0:
            return pltpu.make_async_copy(src, dst, s3or.at[o, 0, n])
        return remote(src, dst, s3os.at[o, step, n], s3or.at[o, step, n], moved(place, three, step), core)

    def across(o, step, n, group, h):
        came = landing(o, (place[WAYS[o][2]] + 4 - step) % 4, group, xo)(h)
        return remote(came, came, fos.at[o, step, n], fors.at[o, step, n], place, 1 - core)

    def group_of(o, n):
        two = WAYS[o][1]
        gap = n ^ (n >> 1)
        return gap, (place[two] + 4 - gap) % 4

    token_lane = lax.broadcasted_iota(jnp.int32, (ROWS, 2 * TOK), 1).astype(F32) + 1.0

    def pack(o, n):
        three = WAYS[o][2]
        gap, group = group_of(o, n)
        column = tab2[o, group].T
        for a in range(4):
            pick = jnp.where(column[:ROWS, a:a + 1] == token_lane, 1.0, 0.0).astype(BF16)
            rows = jnp.dot(pick, gs[o][group, a].reshape(2 * TOK, WIDTH[o]), preferred_element_type=F32)
            rows = rows.astype(BF16)
            rs[o][:, group, a] = rows[:8 * main].reshape(8, main, WIDTH[o])
            if over:
                ro[o][:, group, a] = rows[8 * main:].reshape(4, over, WIDTH[o])
        for step in (1, 3, 2, 0):
            if over:
                third_over(o, step, n, group).start()
            for cc in range(2):
                third(o, step, cc, n, group).start()

    for o in range(3):
        pack(o, 0)
    for back in (0, 1, 3, 2):
        for o in range(3):
            for step in (1, 3):
                second_wait(o, step, back)
                forward(o, step == 1, back).start()

    def others(n, _):
        for o in range(3):
            gap, group = group_of(o, n)

            @pl.when(n == 3)
            def _():
                for back in range(4):
                    forward_wait(o, True, back)
                    forward_wait(o, False, back)

            came = tab2.at[o, group]
            remote(came, came, t2s.at[o, gap], t2r.at[o, gap], place, core).wait_recv()
            pack(o, n)
        return 0

    lax.fori_loop(1, 4, others, 0)

    for o in range(3):
        for step in range(4):
            for cc in range(2):
                if step or cc:
                    first(o, step, cc).wait_send()
                    first_table(o, step, cc).wait_send()
            if step:
                second_table(o, step).wait_send()
        for back in range(4):
            for step in (1, 3):
                second(o, step, back).wait_send()
                forward(o, step == 1, back).wait_send()

    for cp in loads:
        cp.wait()

    def shared_arrive(n, _):
        for o in range(3):
            gap, group = group_of(o, n)
            for step in range(4):
                if step == 0:
                    third_over(o, 0, n, group).wait()
                else:
                    came = landing(o, (place[WAYS[o][2]] + 4 - step) % 4, group, xo)(core)
                    remote(came, came, s3os.at[o, step, n], s3or.at[o, step, n], place, core).wait_recv()
                    third_over(o, step, n, group).wait_send()
                across(o, step, n, group, core).start()
        return 0

    def arrive(n, _):
        for o in range(3):
            three = WAYS[o][2]
            gap, group = group_of(o, n)
            for step in range(4):
                for cc in range(2):
                    came = landing(o, (place[three] + 4 - step) % 4, group, xs)((core + cc) % 2)
                    if step == 0 and cc == 0:
                        third(o, 0, 0, n, group).wait()
                    else:
                        remote(came, came, s3s.at[o, step, cc, n], s3r.at[o, step, cc, n], place, core).wait_recv()
                        third(o, step, cc, n, group).wait_send()
                if over:
                    across(o, step, n, group, core).wait_send()
                    across(o, step, n, group, 1 - core).wait_recv()
        return 0

    if over:
        lax.fori_loop(0, 4, shared_arrive, 0)
    lax.fori_loop(0, 4, arrive, 0)

    for o in range(3):
        for step in range(4):
            for cc in range(2):
                if step or cc:
                    pl.semaphore_signal(
                        free, inc=1, device_id=device(moved(place, WAYS[o][2], step), (core + cc) % 2), device_id_type=MESH
                    )

    mx, my, mz = place

    def send_a(s, x, q, cc, local):
        h = (core + cc) % 2
        src = xs[0].at[h, x, pl.ds(2 * q, 2)]
        dst = rs[0].at[mx * 2 + core, pl.ds(2 * q, 2)]
        if local:
            return pltpu.make_async_copy(src, dst, rar.at[s, cc])
        return remote(src, dst, ras.at[s, cc], rar.at[s, cc], (x, my, mz), h)

    def send_b(s, x, q, i, cc, local):
        h = (core + cc) % 2
        y = 2 * q + (my + i) % 2
        src = xs[1].at[h, x, y]
        dst = rs[1].at[my * 2 + core, :, x]
        if local:
            return pltpu.make_async_copy(src, dst, rbr.at[s, i, cc])
        return remote(src, dst, rbs.at[s, i, cc], rbr.at[s, i, cc], (mx, y, mz), h)

    def send_c(s, x, q, step, cc):
        h = (core + cc) % 2
        z = (mz + step) % 4
        src = xs[2].at[h, x, pl.ds(2 * q, 2), z]
        dst = rs[2].at[mz * 2 + core, x, pl.ds(2 * q, 2)]
        if step == 0 and cc == 0:
            return pltpu.make_async_copy(src, dst, rcr.at[s, 0, 0])
        return remote(src, dst, rcs.at[s, step, cc], rcr.at[s, step, cc], (mx, my, z), h)

    def over_a(s, x, q, local):
        src, dst = xo[0].at[core, x, pl.ds(2 * q, 2)], ro[0].at[mx, pl.ds(2 * q, 2)]
        if local:
            return pltpu.make_async_copy(src, dst, oar.at[s])
        return remote(src, dst, oas.at[s], oar.at[s], (x, my, mz), core)

    def over_b(s, x, q, i, local):
        y = 2 * q + (my + i) % 2
        src, dst = xo[1].at[core, x, y], ro[1].at[my, :, x]
        if local:
            return pltpu.make_async_copy(src, dst, obr.at[s, i])
        return remote(src, dst, obs.at[s, i], obr.at[s, i], (mx, y, mz), core)

    def over_c(s, x, q, step):
        z = (mz + step) % 4
        src, dst = xo[2].at[core, x, pl.ds(2 * q, 2), z], ro[2].at[mz, x, pl.ds(2 * q, 2)]
        if step == 0:
            return pltpu.make_async_copy(src, dst, ocr.at[s, 0])
        return remote(src, dst, ocs.at[s, step], ocr.at[s, step], (mx, my, z), core)

    def each_over(s, o, act):
        x, q = block_of(s)
        if o == 0:
            @pl.when(s % 4 < 3)
            def _():
                act(over_a(s, x, q, False))

            @pl.when(s % 4 == 3)
            def _():
                act(over_a(s, x, q, True))
        elif o == 1:
            act(over_b(s, x, q, 1, False))

            @pl.when(s < 4)
            def _():
                act(over_b(s, x, q, 0, False))

            @pl.when(s >= 4)
            def _():
                act(over_b(s, x, q, 0, True))
        else:
            for step in (1, 3, 2, 0):
                act(over_c(s, x, q, step))

    def to_sibling(s, o):
        x, q = block_of(s)
        return remote(
            xo[o].at[1 - core, x, pl.ds(2 * q, 2)], ys[o].at[x, pl.ds(2 * q, 2)],
            yss.at[s, o], ysr.at[s, o], place, 1 - core,
        )

    def merge(s):
        x, q = block_of(s)
        pair = pl.ds(2 * q, 2)
        for o in range(3):
            to_sibling(s, o).wait_recv()
            mine = xo[o][core, x, pair].reshape(8 * over, WIDTH[o]).astype(F32)
            theirs = ys[o][x, pair].reshape(8 * over, WIDTH[o]).astype(F32)
            kept = jnp.where(hot > 0.0, mine, theirs).astype(BF16)
            xo[o][core, x, pair] = kept.reshape(2, 4, over, WIDTH[o])
            each_over(s, o, lambda cp: cp.start())

    if over:
        me = ((mz * 4 + my) * 4 + mx) * 2 + core
        filled = jnp.where((ids[...] == me) & (slots[...] >= main_slots), 1.0, 0.0)
        hot = jnp.max(jnp.max(filled, axis=1, keepdims=True), axis=0, keepdims=True)

    def block_of(s):
        turn = (s + 1) % 4
        return (mx + (turn ^ (turn >> 1))) % 4, (my // 2 + 1 - s // 4) % 2

    def each(s, o, act):
        x, q = block_of(s)
        for cc in range(2):
            if o == 0 and cc:
                act(send_a(s, x, q, cc, False))
            elif o == 0:
                @pl.when(s % 4 < 3)
                def _():
                    act(send_a(s, x, q, 0, False))

                @pl.when(s % 4 == 3)
                def _():
                    act(send_a(s, x, q, 0, True))
            elif o == 1:
                for i in range(2):
                    if cc or i:
                        act(send_b(s, x, q, i, cc, False))
                    else:
                        @pl.when(s < 4)
                        def _():
                            act(send_b(s, x, q, 0, 0, False))

                        @pl.when(s >= 4)
                        def _():
                            act(send_b(s, x, q, 0, 0, True))
            else:
                for step in (1, 3, 2, 0):
                    act(send_c(s, x, q, step, cc))

    def expert(s, _):
        x, q = block_of(s)
        pair = pl.ds(2 * q, 2)
        halves = [(h, o) for h in range(2) for o in range(3)]
        rows = jnp.concatenate([xs[o][h, x, pair].reshape(8 * main, WIDTH[o]) for h, o in halves], axis=1)
        if over:
            shared = jnp.concatenate([xo[o][h, x, pair].reshape(8 * over, WIDTH[o]) for h, o in halves], axis=1)
            rows = jnp.concatenate([rows, shared], axis=0)
        for f in range(0, FF, 256):
            gate = jnp.dot(rows, wg[:, f:f + 256], preferred_element_type=F32)
            up = jnp.dot(rows, wu[:, f:f + 256], preferred_element_type=F32)
            hidden[:, f:f + 256] = (gate / (1.0 + jnp.exp(-gate)) * up).astype(BF16)
        for h in range(2):
            for o in range(3):
                lo = h * HALF + START[o]
                res = jnp.dot(hidden[...], wd[:, lo:lo + WIDTH[o]], preferred_element_type=F32)
                res = res.astype(BF16)
                xs[o][h, x, pair] = res[:8 * main].reshape(2, 4, main, WIDTH[o])
                if over:
                    xo[o][h, x, pair] = res[8 * main:].reshape(2, 4, over, WIDTH[o])

        @pl.when(s == 0)
        def _():
            pl.semaphore_wait(free, 21)

        for o in range(3):
            if over:
                to_sibling(s, o).start()
            each(s, o, lambda cp: cp.start())
        if over:
            @pl.when(s > 0)
            def _():
                merge(s - 1)
        return 0

    lax.fori_loop(0, 8, expert, 0)
    if over:
        merge(7)

    def returned(o, begin=0, end=8):
        def one_block(s, _):
            each(s, o, lambda cp: cp.wait())
            if over:
                each_over(s, o, lambda cp: cp.wait())
                to_sibling(s, o).wait_send()
            return 0

        lax.fori_loop(begin, end, one_block, 0)

    token_row = lax.broadcasted_iota(jnp.int32, (2 * TOK, ROWS), 0).astype(F32) + 1.0

    FAR, DIRECT, SUM = range(3)

    def push(o, up, kind, turn):
        one, two, _ = WAYS[o]
        step, c = (1, 0) if up else (3, 1)
        a = (place[one] + turn) % 4
        group = (place[two] + (2 if kind == FAR else step)) % 4
        if kind == DIRECT:
            c = 1 - c
        slot = 2 if kind == FAR else step // 2
        at = kind if up else 3 + kind
        return remote(
            gs[o].at[group, a, c], acc2[o].at[slot, a, c],
            q2s.at[o, at, turn], q2r.at[o, at, turn], moved(place, two, step), core,
        )

    def combine(o, step):
        one, two, _ = WAYS[o]
        group = (place[two] + step) % 4
        for turn in (1, 3, 2, 0):
            a = (place[one] + turn) % 4
            index = tab2[o, group, pl.ds(a, 1), :ROWS]
            w = tab2[o, group, pl.ds(4 + a, 1), :ROWS]
            mix = jnp.where(index == token_row, w, 0.0).astype(BF16)
            rows = rs[o][:, group, a].reshape(8 * main, WIDTH[o])
            if over:
                rows = jnp.concatenate([rows, ro[o][:, group, a].reshape(4 * over, WIDTH[o])], axis=0)
            part = jnp.dot(mix, rows, preferred_element_type=F32)
            gs[o][group, a] = part.astype(BF16).reshape(2, TOK, WIDTH[o])
            if step == 2:
                push(o, True, FAR, turn).start()
                push(o, False, FAR, turn).start()
            elif step:
                push(o, step == 1, DIRECT, turn).start()

    returned(0, 0, 4)
    combine(0, 2)
    returned(2)
    for step in (2, 1, 3):
        combine(2, step)
    returned(0, 4, 8)
    returned(1)
    combine(1, 2)
    for step in (1, 3):
        combine(0, step)
        combine(1, step)

    for turn in (1, 3, 2, 0):
        for o in (2, 0, 1):
            one, two, _ = WAYS[o]
            a = (place[one] + turn) % 4
            for up in (True, False):
                step, c = (1, 0) if up else (3, 1)
                group = (place[two] + step) % 4
                push(o, up, FAR, turn).wait_recv()
                gs[o][group, a, c] = (gs[o][group, a, c].astype(F32) + acc2[o][2, a, c].astype(F32)).astype(BF16)
                push(o, up, SUM, turn).start()

    for o in (2, 0, 1):
        combine(o, 0)

    def reduce_first(o, step, cc):
        one, two, _ = WAYS[o]
        c = (core + cc) % 2
        return remote(
            gs[o].at[place[two], (place[one] + step) % 4, c], acc1[o].at[step, cc],
            q1s.at[o, step, cc], q1r.at[o, step, cc], moved(place, one, step), c,
        )

    for step in (1, 3, 2, 0):
        for o in (2, 0, 1):
            one, two, _ = WAYS[o]
            a = (place[one] + step) % 4
            for up in (True, False):
                push(o, up, FAR, step).wait_send()
                push(o, up, DIRECT, step).wait()
                push(o, up, SUM, step).wait()
            total = gs[o][place[two], a].astype(F32)
            for n in range(2):
                total += acc2[o][n, a].astype(F32)
            gs[o][place[two], a] = total.astype(BF16)
            for cc in range(2):
                if step or cc:
                    reduce_first(o, step, cc).start()
            if step == 0:
                acc1[o][0, 0] = gs[o][place[two], place[one], core]

    for o in (2, 0, 1):
        for step in range(4):
            for cc in range(2):
                if step or cc:
                    reduce_first(o, step, cc).wait()
        for cc in range(2):
            h = (core + cc) % 2
            where = pl.ds(pl.multiple_of(h * HALF + START[o], 128), WIDTH[o])
            total = acc1[o][0, cc].astype(F32)
            for step in (1, 2, 3):
                total += acc1[o][step, cc].astype(F32)
            out[:, where] = (resid[:, where].astype(F32) + total).astype(BF16)


def layer(main, over, number, resid, gain, ids, slots, wts, w_gate, w_up, w_down):
    vmem = pl.BlockSpec(memory_space=pltpu.VMEM)
    hbm = pl.BlockSpec(memory_space=pl.ANY)
    lanes = -(-(8 * main + 4 * over) // 128) * 128

    def per_way(*lead, rows):
        return [pltpu.VMEM((*lead, rows, w), BF16) for w in WIDTH]

    def pairs(*shapes):
        return [pltpu.SemaphoreType.DMA(shape) for shape in shapes for _ in range(2)]

    scratch = [
        *per_way(2, rows=TOK),
        *per_way(4, 4, 2, rows=TOK),
        *per_way(8, 4, 4, rows=main),
        *per_way(2, 4, 4, 4, rows=main),
        *per_way(3, 4, 2, rows=TOK),
        *per_way(4, 2, rows=TOK),
        pltpu.VMEM((3, 4, 8, lanes), F32),
        pltpu.VMEM((3, 4, 2, 8, lanes), F32),
        pltpu.VMEM((3, 4, 8, lanes), F32),
        pltpu.VMEM((3, 4, 8, lanes), F32),
        pltpu.VMEM((8 * (main + over), FF), BF16),
        pltpu.VMEM((D, FF), BF16),
        pltpu.VMEM((D, FF), BF16),
        pltpu.VMEM((FF, D), BF16),
        pltpu.SemaphoreType.DMA((3,)),
        *pairs((3, 4, 2), (3, 4, 2), (3, 4, 4), (3, 4), (3, 4, 2, 4), (8, 2), (8, 2, 2), (8, 4, 2), (3, 6, 4), (3, 4, 2)),
        pltpu.SemaphoreType.REGULAR,
    ]
    if over:
        scratch += [
            *per_way(4, 4, 4, rows=over),
            *per_way(2, 4, 4, 4, rows=over),
            *per_way(4, 4, 4, rows=over),
            *pairs((3, 4, 4), (3, 4, 4), (8,), (8, 2), (8, 4), (8, 3)),
        ]
    return pl.pallas_call(
        functools.partial(kernel, main, over),
        out_shape=(jax.ShapeDtypeStruct((TOK, D), BF16), jax.ShapeDtypeStruct((8, 128), F32)) if over
        else jax.ShapeDtypeStruct((TOK, D), BF16),
        in_specs=[vmem] * 5 + [hbm] * 3,
        out_specs=(vmem, vmem) if over else vmem,
        scratch_shapes=scratch,
        compiler_params=pltpu.CompilerParams(
            collective_id=number, has_side_effects=True, vmem_limit_bytes=62 * 2**20
        ),
        cost_estimate=pl.CostEstimate(flops=30 * 10**9, bytes_accessed=11 * 10**6, transcendentals=2 * 10**6),
    )(resid, gain, ids, slots, wts, w_gate, w_up, w_down)


def per_device(resid, norm_gain, w_gate, w_up, w_down, route_ids, route_slots, route_weights):
    args = (
        resid, norm_gain[None, :], route_ids.T, route_slots.T, route_weights.T, w_gate[0], w_up[0], w_down[0],
    )
    result, flag = layer(MAIN, OVER, 0, *args)
    return lax.cond(flag[0, 0] > 0.5, lambda result, *args: layer(2 * CAP, 0, 1, *args), lambda result, *args: result, result, *args)


def solution(mesh):
    rows = P(("dp", "expert"), None)
    expert = P(("dp", "expert"), None, None)
    return jax.shard_map(
        per_device, mesh=mesh, in_specs=(rows, P(), expert, expert, expert, rows, rows, rows), out_specs=rows, check_vma=False
    )
```
